256 devices in a mesh: gx: 8 (over z), gy: 8 (over x, core), gz: 4 (over y).
Axes of the slice: x: 4, y: 4, z: 8, core: 2. Of those that a mesh axis runs over, the one named last changes fastest.
Arguments:
- conserved: float32 [5, 256, 64, 512], P(None, 'gx', 'gy', 'gz'), may hold values from -0.6 to 11, as said below
- gamma_field: float32 [256, 64, 512], P('gx', 'gy', 'gz'), may hold values from 1.2 to 1.67
- species: int32 [256, 64, 512], P('gx', 'gy', 'gz'), may hold values from 0 to 3
- lut_color: float32 [4, 3, 256], replicated, may hold values from 0 to 1
- lut_extinction: float32 [4, 256], replicated, may hold values from 0.0005 to 0.01
Outputs:
- new_state: float32 [5, 256, 64, 512], P(None, 'gx', 'gy', 'gz')
- image_rgba: float32 [4, 1024, 1920], P(None, ('gx', 'gy', 'gz'))
The draws below stay inside these ranges and needn't reach their ends.
Inputs may be any that keep to these rules, and one draw needn't show every extreme that they name: `conserved`: component 0 (density) lies in [0.5, 2]; each velocity component, momentum over density, lies in [-0.3, 0.3]; the pressure computed with gamma_field lies in [0.5, 2].
All inputs are finite; a program needn't handle non-finite values.
Results may differ from the reference program's by a relative error of at most 0.0003.
Values sent between devices are 32-bit elements; how exact they have to be, the bound alone decides.
No kernel may reach another device: no remote copies, remote signals or barrier semaphores. Data moves between devices by JAX's collectives and lax.ppermute only.
A program may use at most 64 MiB of HBM per device.

```python
import math
import jax
import jax.numpy as jnp
from jax import lax

LUT = 256
CLASSES = 4
SW = 1920
ZOOM = 4
NX = 256
NY = 64
NZ = 512


def plume_fields(key):
    base_key = jax.random.fold_in(key, 11)
    subkeys = jax.random.split(base_key, 4)
    extent = (NX, NY, NZ)
    density = jnp.exp(jax.random.uniform(subkeys[0], extent, jnp.float32, math.log(0.5), math.log(2.0)))
    pressure = jnp.exp(jax.random.uniform(subkeys[2], extent, jnp.float32, math.log(0.5), math.log(2.0)))
    velocity = jax.random.uniform(subkeys[1], (3,) + extent, jnp.float32, -0.3, 0.3)
    heat_ratio = jax.random.uniform(subkeys[3], extent, jnp.float32, 1.2, 1.67)
    speed_square = velocity[0] * velocity[0] + velocity[1] * velocity[1] + velocity[2] * velocity[2]
    energy = pressure / (heat_ratio - 1.0) + 0.5 * density * speed_square
    conserved = jnp.stack([density, density * velocity[0], density * velocity[1], density * velocity[2], energy])
    return (conserved, heat_ratio)


def draw_conserved(key, part):
    return plume_fields(key)[0]


def draw_gamma_field(key, part):
    return plume_fields(key)[1]


def touch_ends(entries, rng, low, high):
    place = [jax.random.randint(jax.random.fold_in(rng, axis), (), 0, length) for axis, length in enumerate(entries.shape)]
    main_axis = entries.shape.index(max(entries.shape))
    next_to = place[:main_axis] + [(place[main_axis] + 1) % entries.shape[main_axis]] + place[main_axis + 1:]
    return entries.at[tuple(place)].set(low).at[tuple(next_to)].set(high)


def setup_inputs(seed: int = 0) -> dict:
    arg_keys = jax.random.split(jax.random.key(seed), 6)
    return {
        "conserved": draw_conserved(jax.random.fold_in(arg_keys[5], 71), 0),
        "gamma_field": draw_gamma_field(jax.random.fold_in(arg_keys[5], 71), 0),
        "species": touch_ends(jax.random.randint(arg_keys[2], (NX, NY, NZ), 0, CLASSES), jax.random.fold_in(arg_keys[2], 1), 0, CLASSES - 1).astype(jnp.int32),
        "lut_color": jnp.clip(jax.random.uniform(arg_keys[3], (CLASSES, 3, LUT), jnp.float32, 0.0, 1.0), 0.0, 1.0),
        "lut_extinction": jnp.clip(jnp.exp(jax.random.uniform(arg_keys[4], (CLASSES, LUT), jnp.float32, math.log(0.0005), math.log(0.01))), 0.0005, 0.01),
    }


dissipation = 3.0
courant = 0.11
density_low = 0.6
density_high = 1.6
slab_rows = 8


def divergence(padded, gamma_pad):
    inverse = 1.0 / padded[0]
    momenta = padded[1:4]
    energy = padded[4]
    kinetic = 0.5 * (momenta[0] * momenta[0] + momenta[1] * momenta[1] + momenta[2] * momenta[2]) * inverse
    pressure = (gamma_pad - 1.0) * (energy - kinetic)
    summed = None
    for direction in range(3):
        velocity = momenta[direction] * inverse
        pieces_list = [momenta[direction]]
        for member in range(3):
            component = momenta[member] * velocity
            if member == direction:
                component = component + pressure
            pieces_list.append(component)
        pieces_list.append((energy + pressure) * velocity)
        fluxes = jnp.stack(pieces_list)
        axis_now = direction + 1
        length = padded.shape[axis_now]
        lower_cells = lax.slice_in_dim(padded, 0, length - 1, axis=axis_now)
        upper_cells = lax.slice_in_dim(padded, 1, length, axis=axis_now)
        face_flux = 0.5 * (lax.slice_in_dim(fluxes, 0, length - 1, axis=axis_now) + lax.slice_in_dim(fluxes, 1, length, axis=axis_now)) - 0.5 * dissipation * (upper_cells - lower_cells)
        change = lax.slice_in_dim(face_flux, 1, length - 1, axis=axis_now) - lax.slice_in_dim(face_flux, 0, length - 2, axis=axis_now)
        for other_axis in range(1, 4):
            if other_axis != axis_now:
                change = lax.slice_in_dim(change, 1, change.shape[other_axis] - 1, axis=other_axis)
        summed = change if summed is None else summed + change
    return summed


def advance(widened, gamma_wide):
    halfway = widened[:, 1:-1, 1:-1, 1:-1] - courant * divergence(widened, gamma_wide)
    initial = widened[:, 2:-2, 2:-2, 2:-2]
    return 0.5 * (initial + halfway[:, 1:-1, 1:-1, 1:-1] - courant * divergence(halfway, gamma_wide[1:-1, 1:-1, 1:-1]))


def classify(density, species, lut_table):
    class_count = lut_table.shape[0]
    knots_count = lut_table.shape[2]
    widened_table = jnp.pad(lut_table.transpose(1, 0, 2), ((0, 0), (0, 0), (1, 1)))
    flat_table = widened_table.reshape(4, class_count * (knots_count + 2))
    table_pos = (density - density_low) * ((knots_count - 1) / (density_high - density_low))
    lower_knot = jnp.floor(table_pos)
    fraction = table_pos - lower_knot
    lower_index = jnp.clip(lower_knot + 1.0, 0.0, knots_count + 1.0).astype(jnp.int32)
    upper_index = jnp.clip(lower_knot + 2.0, 0.0, knots_count + 1.0).astype(jnp.int32)
    offset = (species * (knots_count + 2)).astype(jnp.int32)
    lower_vals = jnp.take(flat_table, (offset + lower_index).astype(jnp.int32), axis=1)
    upper_vals = jnp.take(flat_table, (offset + upper_index).astype(jnp.int32), axis=1)
    return (1.0 - fraction)[None] * lower_vals + fraction[None] * upper_vals


def column_planes(properties):
    extinction = properties[3]
    through_sum = jnp.cumsum(extinction, axis=-1)
    before = through_sum - extinction
    transmit = jnp.exp(-before)
    opacity = 1.0 - jnp.exp(-extinction)
    emitted = jnp.sum(properties[:3] * (opacity * transmit)[None], axis=-1)
    through = jnp.exp(-through_sum[..., -1])
    return jnp.concatenate([emitted, through[None]], axis=0)


def warp(planes, screen_width):
    source_rows = planes.shape[1] - 1
    out_rows = jnp.arange(ZOOM * source_rows).astype(jnp.float32) / ZOOM
    vertical = jnp.maximum(0.0, 1.0 - jnp.abs(out_rows[:, None] - jnp.arange(source_rows + 1).astype(jnp.float32)[None, :]))
    columns = planes.shape[2]
    column_pos = jnp.arange(screen_width).astype(jnp.float32) * (columns / screen_width)
    horizontal = jnp.maximum(0.0, 1.0 - jnp.abs(jnp.arange(columns).astype(jnp.float32)[:, None] - column_pos[None, :]))
    stretched = jnp.einsum("ri,civ->crv", vertical, planes, precision=lax.Precision.HIGHEST)
    return jnp.einsum("crv,vs->crs", stretched, horizontal, precision=lax.Precision.HIGHEST)


def reference(conserved, gamma_field, species, lut_color, lut_extinction):
    lut_table = jnp.concatenate([lut_color, lut_extinction[:, None, :]], axis=1)
    slab_count = NX // slab_rows

    def one_slab(slab_index):
        first_row = slab_index * slab_rows
        row_ids = ((first_row - 2 + jnp.arange(slab_rows + 4, dtype=jnp.int32)) % NX).astype(jnp.int32)
        block = jnp.take(conserved, row_ids, axis=1)
        block = jnp.pad(block, ((0, 0), (0, 0), (2, 2), (2, 2)), mode="wrap")
        gamma_block = jnp.pad(jnp.take(gamma_field, row_ids, axis=0), ((0, 0), (2, 2), (2, 2)), mode="wrap")
        updated = advance(block, gamma_block)
        slab_species = lax.dynamic_slice_in_dim(species, first_row.astype(jnp.int32), slab_rows, 0)
        planes = column_planes(classify(updated[0], slab_species, lut_table))
        return updated, planes

    updated_all, planes_all = lax.map(one_slab, jnp.arange(slab_count, dtype=jnp.int32))
    new_state = updated_all.transpose(1, 0, 2, 3, 4).reshape(5, NX, NY, NZ)
    planes = planes_all.transpose(1, 0, 2, 3).reshape(4, NX, NY)
    visible = jnp.concatenate([planes[:3], 1.0 - planes[3:]], axis=0)
    stacked = jnp.concatenate([visible, jnp.zeros((4, 1, NY), jnp.float32)], axis=1)
    return new_state, warp(stacked, SW)
```

```python
import functools

import jax
import jax.numpy as jnp
from jax import lax
from jax.experimental import pallas as pl
from jax.experimental.pallas import tpu as pltpu
from jax.sharding import PartitionSpec as P

SW = 1920
ZOOM = 4
CLASSES = 4
LUT = 256

dissipation = 3.0
courant = 0.11
density_low = 0.6
density_high = 1.6

F32 = jnp.float32
LANES = 128
SUBS = 8
VMEM_LIMIT = 48 * 1024 * 1024


def iota(shape, dim):
    return lax.broadcasted_iota(jnp.int32, shape, dim)


def halves(direction, cell):
    density, m1, m2, m3, energy, gamma = cell
    momenta = (m1, m2, m3)
    inverse = 1.0 / density
    kinetic = 0.5 * (m1 * m1 + m2 * m2 + m3 * m3) * inverse
    pressure = (gamma - 1.0) * (energy - kinetic)
    half_p = 0.5 * pressure
    scaled = [(0.5 * dissipation) * q for q in (density, m1, m2, m3, energy)]
    result = []
    for d in direction:
        half_v = 0.5 * momenta[d] * inverse
        flux = [0.5 * momenta[d]]
        for member in range(3):
            component = momenta[member] * half_v
            flux.append(component + half_p if member == d else component)
        flux.append((energy + pressure) * half_v)
        result.append(
            ([a - b for a, b in zip(flux, scaled)], [a + b for a, b in zip(flux, scaled)])
        )
    return result


def prepare_halo(ym, yp, zm, zp, gym, gyp, gzm, gzp, y_below, y_above, z_edge):
    below = halves((1,), [ym[f] for f in range(5)] + [gym])[0][1]
    above = halves((1,), [yp[f] for f in range(5)] + [gyp])[0][0]
    for f in range(5):
        y_below[f] = below[f]
        y_above[f] = above[f]
    z_lower = [pltpu.roll(zm[f], 1, 1) for f in range(5)] + [pltpu.roll(gzm, 1, 1)]
    z_upper = [pltpu.roll(zp[f], LANES - 1, 1) for f in range(5)] + [
        pltpu.roll(gzp, LANES - 1, 1)
    ]
    odd = iota((SUBS, LANES), 1) % 2 == 1
    merged = [jnp.where(odd, a, b) for a, b in zip(z_lower, z_upper)]
    merged = [jnp.where(iota((SUBS, LANES), 1) < 64, q, 1.0) for q in merged]
    up, down = halves((2,), merged)[0]
    for f in range(5):
        z_edge[f] = jnp.where(odd, down[f], up[f])


def row_terms(cell, row, y_below, y_above, z_edge):
    lane = iota((SUBS, LANES), 1)
    sub = iota((SUBS, LANES), 0)
    (x_up, x_down), (y_up, y_down), (z_up, z_down) = halves((0, 1, 2), cell)
    core = []
    for f in range(5):
        edge = pltpu.roll(z_edge[f], LANES - 1 - 2 * row, 1)
        from_above = jnp.where(lane == LANES - 1, edge, pltpu.roll(z_up[f], LANES - 1, 1))
        from_below = jnp.where(lane == 0, edge, pltpu.roll(z_down[f], 1, 1))
        total = 6.0 * (0.5 * dissipation) * cell[f] + (from_above - from_below)
        from_above = jnp.where(
            sub == SUBS - 1, y_above[f, pl.ds(row, 1), :], pltpu.roll(y_up[f], SUBS - 1, 0)
        )
        from_below = jnp.where(
            sub == 0, y_below[f, pl.ds(row, 1), :], pltpu.roll(y_down[f], 1, 0)
        )
        core.append(total + (from_above - from_below))
    return x_up, x_down, core


def walk(rows, load, x_first, x_last, finish, y_below, y_above, z_edge):
    down_before = halves((0,), x_first)[0][1]
    up_after = halves((0,), x_last)[0][0]

    def step(row, carry, emit):
        pending, down = carry
        x_up, x_down, core = row_terms(load(row), row, y_below, y_above, z_edge)
        if emit:
            finish(row - 1, [a + b for a, b in zip(pending, x_up)])
        return [a - b for a, b in zip(core, down)], x_down

    carry = step(0, (None, down_before), False)
    carry = lax.fori_loop(1, rows, lambda row, c: step(row, c, True), carry)
    finish(rows - 1, [a + b for a, b in zip(carry[0], up_after)])


def put_faces(f, row, rows, value, y_low, y_high, z_pack):
    y_low[f, pl.ds(row, 1), :] = value[0:1, :]
    y_high[f, pl.ds(row, 1), :] = value[SUBS - 1 : SUBS, :]
    lane = iota((SUBS, LANES), 1)
    z_pack[f] = jnp.where(lane // 2 == row, pltpu.roll(value, 2 * row + 1, 1), z_pack[f])


def pack_kernel(u, g, x_low, x_high, y_low, y_high, z_pack):
    rows = u.shape[1]
    z_pack[...] = jnp.zeros(z_pack.shape, F32)
    for f in range(6):
        x_low[f] = u[f, 0] if f < 5 else g[0]
        x_high[f] = u[f, rows - 1] if f < 5 else g[rows - 1]

    def body(row, _):
        for f in range(6):
            put_faces(f, row, rows, u[f, row] if f < 5 else g[row], y_low, y_high, z_pack)
        return 0

    lax.fori_loop(0, rows, body, 0)


def half_kernel(
    u, g, xm, xp, ym, yp, zm, zp, h, x_low, x_high, y_low, y_high, z_pack, y_below, y_above, z_edge
):
    rows = u.shape[1]
    prepare_halo(ym, yp, zm, zp, ym[5], yp[5], zm[5], zp[5], y_below, y_above, z_edge)
    z_pack[...] = jnp.zeros(z_pack.shape, F32)

    def load(row):
        return [u[f, row] for f in range(5)] + [g[row]]

    def finish(row, change):
        for f in range(5):
            value = u[f, row] - courant * change[f]
            h[f, row] = value
            put_faces(f, row, rows, value, y_low, y_high, z_pack)

    walk(
        rows,
        load,
        [xm[f] for f in range(6)],
        [xp[f] for f in range(6)],
        finish,
        y_below,
        y_above,
        z_edge,
    )
    for f in range(5):
        x_low[f] = h[f, 0]
        x_high[f] = h[f, rows - 1]


def lookup(density, species, tables):
    position = (density - density_low) * ((LUT - 1) / (density_high - density_low))
    knot = jnp.clip(jnp.floor(position), 0.0, LUT - 1.0)
    offset = position - knot
    lower_weight = jnp.maximum(0.0, 1.0 - jnp.abs(offset))
    upper_weight = jnp.maximum(0.0, 1.0 - jnp.abs(offset - 1.0))
    index = knot.astype(jnp.int32)
    lane_index = index % LANES
    bits = (index >= LANES, species % 2 == 1, species >= 2)
    result = []
    for channel in range(4):
        total = None
        for side, weight in ((0, lower_weight), (1, upper_weight)):
            values = [
                jnp.take_along_axis(
                    tables[channel, side, k], lane_index, axis=1, mode="promise_in_bounds"
                )
                for k in range(8)
            ]
            for bit in bits:
                values = [
                    jnp.where(bit, values[k + 1], values[k]) for k in range(0, len(values), 2)
                ]
            term = weight * values[0]
            total = term if total is None else total + term
        result.append(total)
    return result


def spread_tables(lut_lower, lut_upper, tables):
    for channel in range(4):
        for k in range(8):
            for side, source in ((0, lut_lower), (1, lut_upper)):
                row = source[pl.ds(channel * 8 + k, 1), :]
                tables[channel, side, k] = jnp.broadcast_to(row, (SUBS, LANES))


def split_dot(value, weights):
    first = value.astype(jnp.bfloat16)
    rest = value - first.astype(F32)
    second = rest.astype(jnp.bfloat16)
    third = (rest - second.astype(F32)).astype(jnp.bfloat16)
    total = jnp.dot(first, weights, preferred_element_type=F32)
    total += jnp.dot(second, weights, preferred_element_type=F32)
    return total + jnp.dot(third, weights, preferred_element_type=F32)


def integrate(properties, planes, rows):
    extinction = properties[3]
    below = (iota((LANES, LANES), 0) < iota((LANES, LANES), 1)).astype(jnp.bfloat16)
    before = split_dot(extinction, below)
    factor = (1.0 - jnp.exp(-extinction)) * jnp.exp(-before)
    lane = iota((SUBS, LANES), 1)
    gathered = []
    for channel in range(4):
        if channel < 3:
            weighted = properties[channel] * factor
        else:
            weighted = extinction
        summed = jnp.sum(weighted, axis=1, keepdims=True)
        if channel == 3:
            summed = jnp.exp(-summed)
        plane = jnp.zeros((SUBS, LANES), F32)
        for row in range(rows):
            plane = jnp.where(lane == row, summed[row * SUBS : (row + 1) * SUBS], plane)
        gathered.append(plane)
    block = jnp.concatenate(gathered + [jnp.zeros((LANES - 32, LANES), F32)], axis=0)
    planes[...] = jnp.transpose(block)[:rows]


def step_kernel(
    u, g, sp, h, gxm, gxp, gym, gyp, gzm, gzp, xm, xp, ym, yp, zm, zp, lut_lower, lut_upper,
    new, planes, y_below, y_above, z_edge, tables, properties
):
    rows = u.shape[1]
    spread_tables(lut_lower, lut_upper, tables)
    prepare_halo(ym, yp, zm, zp, gym[...], gyp[...], gzm[...], gzp[...], y_below, y_above, z_edge)

    def load(row):
        return [h[f, row] for f in range(5)] + [g[row]]

    def finish(row, change):
        for f in range(5):
            value = 0.5 * (u[f, row] + h[f, row] - courant * change[f])
            new[f, row] = value
            if f == 0:
                density = value
        found = lookup(density, sp[row], tables)
        for channel in range(4):
            properties[channel, pl.ds(pl.multiple_of(row * SUBS, SUBS), SUBS), :] = found[channel]

    walk(
        rows,
        load,
        [xm[f] for f in range(5)] + [gxm[...]],
        [xp[f] for f in range(5)] + [gxp[...]],
        finish,
        y_below,
        y_above,
        z_edge,
    )
    integrate(properties, planes, rows)


def image_kernel(across_y, across_z, flags, parts, out):
    lane = iota((across_y, LANES), 1)
    channel = (lane // 8) % 4
    total = None
    for k in reversed(range(across_z)):
        part = parts[pl.ds(k, across_y, stride=across_z), :]
        through = part
        for c in range(3):
            moved = pltpu.roll(part, LANES - (24 - 8 * c), 1)
            through = jnp.where(channel == c, moved, through)
        if total is None:
            total = part
        else:
            total = jnp.where(channel == 3, 0.0, part) + through * total
    total = jnp.where(channel == 3, 1.0 - total, total)
    keep = jnp.where(lane >= 32, flags[0], 1.0)
    total = jnp.where(lane < 64, total * keep, 0.0)
    sub8 = iota((8, LANES), 0)
    lane8 = iota((8, LANES), 1)
    moved = jnp.zeros((8, LANES), F32)
    for k in range(across_y):
        wide = jnp.broadcast_to(total[k : k + 1, :], (8, LANES))
        shifted = wide
        for bit in range(3):
            amount = (LANES - (8 << bit)) % LANES
            shifted = jnp.where(
                (sub8 >> bit) & 1 == 1, pltpu.roll(shifted, amount, 1), shifted
            )
        if k:
            shifted = pltpu.roll(shifted, 8 * k, 1)
        moved = jnp.where(lane8 // 8 == k, shifted, moved)
    columns = 8 * across_y
    screen = jnp.concatenate(
        [
            (1.0 - q / ZOOM) * moved[c : c + 1, :columns]
            + (q / ZOOM) * moved[4 + c : 5 + c, :columns]
            for c in range(4)
            for q in range(ZOOM)
        ],
        axis=0,
    )
    position = iota((columns, SW), 1).astype(F32) * (columns / SW)
    horizontal = jnp.maximum(
        0.0, 1.0 - jnp.abs(iota((columns, SW), 0).astype(F32) - position)
    )
    image = jnp.dot(
        screen, horizontal, precision=lax.Precision.HIGHEST, preferred_element_type=F32
    )
    for c in range(4):
        out[c] = image[c * ZOOM : (c + 1) * ZOOM]


def shifted(value, axis, steps):
    size = lax.axis_size(axis)
    return lax.ppermute(value, axis, [(i, (i + steps) % size) for i in range(size)])


def exchange(x_low, x_high, y_low, y_high, z_pack):
    return (
        shifted(x_high, "gx", 1),
        shifted(x_low, "gx", -1),
        shifted(y_high, "gy", 1),
        shifted(y_low, "gy", -1),
        shifted(z_pack, "gz", 1),
        shifted(z_pack, "gz", -1),
    )


def struct(*shape):
    return jax.ShapeDtypeStruct(shape, F32)


def faces(fields, rows):
    return (
        struct(fields, SUBS, LANES),
        struct(fields, SUBS, LANES),
        struct(fields, rows, LANES),
        struct(fields, rows, LANES),
        struct(fields, SUBS, LANES),
    )


def local(conserved, gamma_field, species, lut_color, lut_extinction):
    rows = conserved.shape[1]
    params = pltpu.CompilerParams(vmem_limit_bytes=VMEM_LIMIT)
    halo_scratch = [
        pltpu.VMEM((5, rows, LANES), F32),
        pltpu.VMEM((5, rows, LANES), F32),
        pltpu.VMEM((5, SUBS, LANES), F32),
    ]
    across_y = lax.axis_size("gy")
    across_z = lax.axis_size("gz")

    lut_table = jnp.concatenate([lut_color, lut_extinction[:, None, :]], axis=1)
    lut_lower = lut_table.transpose(1, 0, 2).reshape(32, LANES)
    lut_upper = (
        jnp.pad(lut_table[:, :, 1:], ((0, 0), (0, 0), (0, 1))).transpose(1, 0, 2).reshape(32, LANES)
    )

    first = exchange(
        *pl.pallas_call(pack_kernel, out_shape=faces(6, rows), compiler_params=params, name="pack")(
            conserved, gamma_field
        )
    )
    halfway, *edges = pl.pallas_call(
        half_kernel,
        out_shape=(struct(*conserved.shape),) + faces(5, rows),
        scratch_shapes=halo_scratch,
        compiler_params=params,
        name="half",
    )(conserved, gamma_field, *first)
    second = exchange(*edges)
    new_state, planes = pl.pallas_call(
        step_kernel,
        out_shape=(struct(*conserved.shape), struct(rows, LANES)),
        scratch_shapes=halo_scratch
        + [
            pltpu.VMEM((4, 2, 8, SUBS, LANES), F32),
            pltpu.VMEM((4, rows * SUBS, LANES), F32),
        ],
        compiler_params=params,
        name="step",
    )(
        conserved,
        gamma_field,
        species,
        halfway,
        *[part[5] for part in first],
        *second,
        lut_lower,
        lut_upper,
    )
    next_first = shifted(planes[:1], "gx", -1)
    below = jnp.concatenate([planes[1:], next_first], axis=0)
    grouped = jnp.concatenate(
        [planes[:, :32], below[:, :32], jnp.zeros((rows, 64), F32)], axis=1
    )
    merged = lax.all_to_all(
        grouped.reshape(across_y * across_z, 1, LANES), ("gy", "gz"), 0, 0, tiled=True
    ).reshape(across_y * across_z, LANES)
    place = lax.axis_index(("gx", "gy", "gz"))
    last = lax.axis_size(("gx", "gy", "gz")) - 1
    flags = jnp.where(place == last, 0.0, 1.0).reshape(1)
    image = pl.pallas_call(
        functools.partial(image_kernel, across_y, across_z),
        out_shape=struct(4, ZOOM, SW),
        in_specs=[
            pl.BlockSpec(memory_space=pltpu.SMEM),
            pl.BlockSpec(memory_space=pltpu.VMEM),
        ],
        compiler_params=params,
        name="image",
    )(flags, merged)
    return new_state, image


def solution(mesh):
    return jax.shard_map(
        local,
        mesh=mesh,
        in_specs=(P(None, "gx", "gy", "gz"), P("gx", "gy", "gz"), P("gx", "gy", "gz"), P(), P()),
        out_specs=(P(None, "gx", "gy", "gz"), P(None, ("gx", "gy", "gz"), None)),
        check_vma=False,
    )
```

```python
import functools

import jax
import jax.numpy as jnp
from jax import lax
from jax.experimental import pallas as pl
from jax.experimental.pallas import tpu as pltpu
from jax.sharding import PartitionSpec as P

SW = 1920
ZOOM = 4
CLASSES = 4
LUT = 256

dissipation = 3.0
courant = 0.11
density_low = 0.6
density_high = 1.6

F32 = jnp.float32
LANES = 128
SUBS = 8
VMEM_LIMIT = 48 * 1024 * 1024


def iota(shape, dim):
    return lax.broadcasted_iota(jnp.int32, shape, dim)


def halves(direction, cell):
    density, m1, m2, m3, energy, gamma = cell
    momenta = (m1, m2, m3)
    inverse = 1.0 / density
    kinetic = 0.5 * (m1 * m1 + m2 * m2 + m3 * m3) * inverse
    pressure = (gamma - 1.0) * (energy - kinetic)
    half_p = 0.5 * pressure
    scaled = [(0.5 * dissipation) * q for q in (density, m1, m2, m3, energy)]
    result = []
    for d in direction:
        half_v = 0.5 * momenta[d] * inverse
        flux = [0.5 * momenta[d]]
        for member in range(3):
            component = momenta[member] * half_v
            flux.append(component + half_p if member == d else component)
        flux.append((energy + pressure) * half_v)
        result.append(
            ([a - b for a, b in zip(flux, scaled)], [a + b for a, b in zip(flux, scaled)])
        )
    return result


def prepare_halo(ym, yp, zm, zp, gym, gyp, gzm, gzp, y_below, y_above, z_edge):
    below = halves((1,), [ym[f] for f in range(5)] + [gym])[0][1]
    above = halves((1,), [yp[f] for f in range(5)] + [gyp])[0][0]
    for f in range(5):
        y_below[f] = below[f]
        y_above[f] = above[f]
    z_lower = [pltpu.roll(zm[f], 1, 1) for f in range(5)] + [pltpu.roll(gzm, 1, 1)]
    z_upper = [pltpu.roll(zp[f], LANES - 1, 1) for f in range(5)] + [
        pltpu.roll(gzp, LANES - 1, 1)
    ]
    odd = iota((SUBS, LANES), 1) % 2 == 1
    merged = [jnp.where(odd, a, b) for a, b in zip(z_lower, z_upper)]
    merged = [jnp.where(iota((SUBS, LANES), 1) < 64, q, 1.0) for q in merged]
    up, down = halves((2,), merged)[0]
    for f in range(5):
        z_edge[f] = jnp.where(odd, down[f], up[f])


def row_terms(cell, row, y_below, y_above, z_edge):
    lane = iota((SUBS, LANES), 1)
    sub = iota((SUBS, LANES), 0)
    (x_up, x_down), (y_up, y_down), (z_up, z_down) = halves((0, 1, 2), cell)
    core = []
    for f in range(5):
        edge = pltpu.roll(z_edge[f], LANES - 1 - 2 * row, 1)
        from_above = jnp.where(lane == LANES - 1, edge, pltpu.roll(z_up[f], LANES - 1, 1))
        from_below = jnp.where(lane == 0, edge, pltpu.roll(z_down[f], 1, 1))
        total = 6.0 * (0.5 * dissipation) * cell[f] + (from_above - from_below)
        from_above = jnp.where(
            sub == SUBS - 1, y_above[f, pl.ds(row, 1), :], pltpu.roll(y_up[f], SUBS - 1, 0)
        )
        from_below = jnp.where(
            sub == 0, y_below[f, pl.ds(row, 1), :], pltpu.roll(y_down[f], 1, 0)
        )
        core.append(total + (from_above - from_below))
    return x_up, x_down, core


def walk(rows, load, x_first, x_last, finish, y_below, y_above, z_edge):
    down_before = halves((0,), x_first)[0][1]
    up_after = halves((0,), x_last)[0][0]

    def step(row, carry, emit):
        pending, down = carry
        x_up, x_down, core = row_terms(load(row), row, y_below, y_above, z_edge)
        if emit:
            finish(row - 1, [a + b for a, b in zip(pending, x_up)])
        return [a - b for a, b in zip(core, down)], x_down

    carry = step(0, (None, down_before), False)
    carry = lax.fori_loop(1, rows, lambda row, c: step(row, c, True), carry, unroll=True)
    finish(rows - 1, [a + b for a, b in zip(carry[0], up_after)])


def put_faces(f, row, rows, value, y_low, y_high, z_pack):
    y_low[f, pl.ds(row, 1), :] = value[0:1, :]
    y_high[f, pl.ds(row, 1), :] = value[SUBS - 1 : SUBS, :]
    lane = iota((SUBS, LANES), 1)
    z_pack[f] = jnp.where(lane // 2 == row, pltpu.roll(value, 2 * row + 1, 1), z_pack[f])


def pack_kernel(u, g, x_low, x_high, y_low, y_high, z_pack):
    rows = u.shape[1]
    z_pack[...] = jnp.zeros(z_pack.shape, F32)
    for f in range(6):
        x_low[f] = u[f, 0] if f < 5 else g[0]
        x_high[f] = u[f, rows - 1] if f < 5 else g[rows - 1]

    def body(row, _):
        for f in range(6):
            put_faces(f, row, rows, u[f, row] if f < 5 else g[row], y_low, y_high, z_pack)
        return 0

    lax.fori_loop(0, rows, body, 0, unroll=True)


def half_kernel(
    u, g, xm, xp, ym, yp, zm, zp, h, x_low, x_high, y_low, y_high, z_pack, y_below, y_above, z_edge
):
    rows = u.shape[1]
    prepare_halo(ym, yp, zm, zp, ym[5], yp[5], zm[5], zp[5], y_below, y_above, z_edge)
    z_pack[...] = jnp.zeros(z_pack.shape, F32)

    def load(row):
        return [u[f, row] for f in range(5)] + [g[row]]

    def finish(row, change):
        for f in range(5):
            value = u[f, row] - courant * change[f]
            h[f, row] = value
            put_faces(f, row, rows, value, y_low, y_high, z_pack)

    walk(
        rows,
        load,
        [xm[f] for f in range(6)],
        [xp[f] for f in range(6)],
        finish,
        y_below,
        y_above,
        z_edge,
    )
    for f in range(5):
        x_low[f] = h[f, 0]
        x_high[f] = h[f, rows - 1]


def lookup(density, species, tables):
    position = (density - density_low) * ((LUT - 1) / (density_high - density_low))
    knot = jnp.clip(jnp.floor(position), 0.0, LUT - 1.0)
    offset = position - knot
    lower_weight = jnp.maximum(0.0, 1.0 - jnp.abs(offset))
    upper_weight = jnp.maximum(0.0, 1.0 - jnp.abs(offset - 1.0))
    index = knot.astype(jnp.int32)
    lane_index = index % LANES
    bits = (index >= LANES, species % 2 == 1, species >= 2)
    result = []
    for channel in range(4):
        total = None
        for side, weight in ((0, lower_weight), (1, upper_weight)):
            values = [
                jnp.take_along_axis(
                    tables[channel, side, k], lane_index, axis=1, mode="promise_in_bounds"
                )
                for k in range(8)
            ]
            for bit in bits:
                values = [
                    jnp.where(bit, values[k + 1], values[k]) for k in range(0, len(values), 2)
                ]
            term = weight * values[0]
            total = term if total is None else total + term
        result.append(total)
    return result


def spread_tables(lut_lower, lut_upper, tables):
    for channel in range(4):
        for k in range(8):
            for side, source in ((0, lut_lower), (1, lut_upper)):
                row = source[pl.ds(channel * 8 + k, 1), :]
                tables[channel, side, k] = jnp.broadcast_to(row, (SUBS, LANES))


def split_dot(value, weights):
    first = value.astype(jnp.bfloat16)
    rest = value - first.astype(F32)
    second = rest.astype(jnp.bfloat16)
    third = (rest - second.astype(F32)).astype(jnp.bfloat16)
    total = jnp.dot(first, weights, preferred_element_type=F32)
    total += jnp.dot(second, weights, preferred_element_type=F32)
    return total + jnp.dot(third, weights, preferred_element_type=F32)


def integrate(properties, planes, rows):
    extinction = properties[3]
    below = (iota((LANES, LANES), 0) < iota((LANES, LANES), 1)).astype(jnp.bfloat16)
    before = split_dot(extinction, below)
    factor = (1.0 - jnp.exp(-extinction)) * jnp.exp(-before)
    lane = iota((SUBS, LANES), 1)
    gathered = []
    for channel in range(4):
        if channel < 3:
            weighted = properties[channel] * factor
        else:
            weighted = extinction
        summed = jnp.sum(weighted, axis=1, keepdims=True)
        if channel == 3:
            summed = jnp.exp(-summed)
        plane = jnp.zeros((SUBS, LANES), F32)
        for row in range(rows):
            plane = jnp.where(lane == row, summed[row * SUBS : (row + 1) * SUBS], plane)
        gathered.append(plane)
    block = jnp.concatenate(gathered + [jnp.zeros((LANES - 32, LANES), F32)], axis=0)
    planes[...] = jnp.transpose(block)[:rows]


def step_kernel(
    u, g, sp, h, gxm, gxp, gym, gyp, gzm, gzp, xm, xp, ym, yp, zm, zp, lut_lower, lut_upper,
    new, planes, y_below, y_above, z_edge, tables, properties
):
    rows = u.shape[1]
    spread_tables(lut_lower, lut_upper, tables)
    prepare_halo(ym, yp, zm, zp, gym[...], gyp[...], gzm[...], gzp[...], y_below, y_above, z_edge)

    def load(row):
        return [h[f, row] for f in range(5)] + [g[row]]

    def finish(row, change):
        for f in range(5):
            value = 0.5 * (u[f, row] + h[f, row] - courant * change[f])
            new[f, row] = value
            if f == 0:
                density = value
        found = lookup(density, sp[row], tables)
        for channel in range(4):
            properties[channel, pl.ds(pl.multiple_of(row * SUBS, SUBS), SUBS), :] = found[channel]

    walk(
        rows,
        load,
        [xm[f] for f in range(5)] + [gxm[...]],
        [xp[f] for f in range(5)] + [gxp[...]],
        finish,
        y_below,
        y_above,
        z_edge,
    )
    integrate(properties, planes, rows)


def image_kernel(across_y, across_z, flags, parts, out):
    lane = iota((across_y, LANES), 1)
    channel = (lane // 8) % 4
    total = None
    for k in reversed(range(across_z)):
        part = parts[pl.ds(k, across_y, stride=across_z), :]
        through = part
        for c in range(3):
            moved = pltpu.roll(part, LANES - (24 - 8 * c), 1)
            through = jnp.where(channel == c, moved, through)
        if total is None:
            total = part
        else:
            total = jnp.where(channel == 3, 0.0, part) + through * total
    total = jnp.where(channel == 3, 1.0 - total, total)
    keep = jnp.where(lane >= 32, flags[0], 1.0)
    total = jnp.where(lane < 64, total * keep, 0.0)
    sub8 = iota((8, LANES), 0)
    lane8 = iota((8, LANES), 1)
    moved = jnp.zeros((8, LANES), F32)
    for k in range(across_y):
        wide = jnp.broadcast_to(total[k : k + 1, :], (8, LANES))
        shifted = wide
        for bit in range(3):
            amount = (LANES - (8 << bit)) % LANES
            shifted = jnp.where(
                (sub8 >> bit) & 1 == 1, pltpu.roll(shifted, amount, 1), shifted
            )
        if k:
            shifted = pltpu.roll(shifted, 8 * k, 1)
        moved = jnp.where(lane8 // 8 == k, shifted, moved)
    columns = 8 * across_y
    screen = jnp.concatenate(
        [
            (1.0 - q / ZOOM) * moved[c : c + 1, :columns]
            + (q / ZOOM) * moved[4 + c : 5 + c, :columns]
            for c in range(4)
            for q in range(ZOOM)
        ],
        axis=0,
    )
    position = iota((columns, SW), 1).astype(F32) * (columns / SW)
    horizontal = jnp.maximum(
        0.0, 1.0 - jnp.abs(iota((columns, SW), 0).astype(F32) - position)
    )
    image = jnp.dot(
        screen, horizontal, precision=lax.Precision.HIGHEST, preferred_element_type=F32
    )
    for c in range(4):
        out[c] = image[c * ZOOM : (c + 1) * ZOOM]


def shifted(value, axis, steps):
    size = lax.axis_size(axis)
    return lax.ppermute(value, axis, [(i, (i + steps) % size) for i in range(size)])


def exchange(x_low, x_high, y_low, y_high, z_pack):
    return (
        shifted(x_high, "gx", 1),
        shifted(x_low, "gx", -1),
        shifted(y_high, "gy", 1),
        shifted(y_low, "gy", -1),
        shifted(z_pack, "gz", 1),
        shifted(z_pack, "gz", -1),
    )


def struct(*shape):
    return jax.ShapeDtypeStruct(shape, F32)


def faces(fields, rows):
    return (
        struct(fields, SUBS, LANES),
        struct(fields, SUBS, LANES),
        struct(fields, rows, LANES),
        struct(fields, rows, LANES),
        struct(fields, SUBS, LANES),
    )


def local(conserved, gamma_field, species, lut_color, lut_extinction):
    rows = conserved.shape[1]
    params = pltpu.CompilerParams(vmem_limit_bytes=VMEM_LIMIT)
    halo_scratch = [
        pltpu.VMEM((5, rows, LANES), F32),
        pltpu.VMEM((5, rows, LANES), F32),
        pltpu.VMEM((5, SUBS, LANES), F32),
    ]
    across_y = lax.axis_size("gy")
    across_z = lax.axis_size("gz")

    lut_table = jnp.concatenate([lut_color, lut_extinction[:, None, :]], axis=1)
    lut_lower = lut_table.transpose(1, 0, 2).reshape(32, LANES)
    lut_upper = (
        jnp.pad(lut_table[:, :, 1:], ((0, 0), (0, 0), (0, 1))).transpose(1, 0, 2).reshape(32, LANES)
    )

    first = exchange(
        *pl.pallas_call(pack_kernel, out_shape=faces(6, rows), compiler_params=params, name="pack")(
            conserved, gamma_field
        )
    )
    halfway, *edges = pl.pallas_call(
        half_kernel,
        out_shape=(struct(*conserved.shape),) + faces(5, rows),
        scratch_shapes=halo_scratch,
        compiler_params=params,
        name="half",
    )(conserved, gamma_field, *first)
    second = exchange(*edges)
    new_state, planes = pl.pallas_call(
        step_kernel,
        out_shape=(struct(*conserved.shape), struct(rows, LANES)),
        scratch_shapes=halo_scratch
        + [
            pltpu.VMEM((4, 2, 8, SUBS, LANES), F32),
            pltpu.VMEM((4, rows * SUBS, LANES), F32),
        ],
        compiler_params=params,
        name="step",
    )(
        conserved,
        gamma_field,
        species,
        halfway,
        *[part[5] for part in first],
        *second,
        lut_lower,
        lut_upper,
    )
    next_first = shifted(planes[:1], "gx", -1)
    below = jnp.concatenate([planes[1:], next_first], axis=0)
    grouped = jnp.concatenate(
        [planes[:, :32], below[:, :32], jnp.zeros((rows, 64), F32)], axis=1
    )
    merged = lax.all_to_all(
        grouped.reshape(across_y * across_z, 1, LANES), ("gy", "gz"), 0, 0, tiled=True
    ).reshape(across_y * across_z, LANES)
    place = lax.axis_index(("gx", "gy", "gz"))
    last = lax.axis_size(("gx", "gy", "gz")) - 1
    flags = jnp.where(place == last, 0.0, 1.0).reshape(1)
    image = pl.pallas_call(
        functools.partial(image_kernel, across_y, across_z),
        out_shape=struct(4, ZOOM, SW),
        in_specs=[
            pl.BlockSpec(memory_space=pltpu.SMEM),
            pl.BlockSpec(memory_space=pltpu.VMEM),
        ],
        compiler_params=params,
        name="image",
    )(flags, merged)
    return new_state, image


def solution(mesh):
    return jax.shard_map(
        local,
        mesh=mesh,
        in_specs=(P(None, "gx", "gy", "gz"), P("gx", "gy", "gz"), P("gx", "gy", "gz"), P(), P()),
        out_specs=(P(None, "gx", "gy", "gz"), P(None, ("gx", "gy", "gz"), None)),
        check_vma=False,
    )
```

```python
import functools

import jax
import jax.numpy as jnp
from jax import lax
from jax.experimental import pallas as pl
from jax.experimental.pallas import tpu as pltpu
from jax.sharding import PartitionSpec as P

SW = 1920
ZOOM = 4
CLASSES = 4
LUT = 256

dissipation = 3.0
courant = 0.11
density_low = 0.6
density_high = 1.6

F32 = jnp.float32
LANES = 128
SUBS = 8
VMEM_LIMIT = 48 * 1024 * 1024


def iota(shape, dim):
    return lax.broadcasted_iota(jnp.int32, shape, dim)


def halves(direction, cell):
    density, m1, m2, m3, energy, gamma = cell
    momenta = (m1, m2, m3)
    inverse = 1.0 / density
    kinetic = 0.5 * (m1 * m1 + m2 * m2 + m3 * m3) * inverse
    pressure = (gamma - 1.0) * (energy - kinetic)
    half_p = 0.5 * pressure
    scaled = [(0.5 * dissipation) * q for q in (density, m1, m2, m3, energy)]
    result = []
    for d in direction:
        half_v = 0.5 * momenta[d] * inverse
        flux = [0.5 * momenta[d]]
        for member in range(3):
            component = momenta[member] * half_v
            flux.append(component + half_p if member == d else component)
        flux.append((energy + pressure) * half_v)
        result.append(
            ([a - b for a, b in zip(flux, scaled)], [a + b for a, b in zip(flux, scaled)])
        )
    return result


def up_of(direction, cell):
    return halves((direction,), cell)[0][0]


def down_of(direction, cell):
    return halves((direction,), cell)[0][1]


def total_change(cell, pairs):
    result = []
    for f in range(5):
        total = (6.0 * 0.5 * dissipation) * cell[f]
        for above, below in pairs:
            total = total + (above[f] - below[f])
        result.append(total)
    return result


def lanes():
    return iota((SUBS, LANES), 1)


def subs():
    return iota((SUBS, LANES), 0)


def along_y(up, down, below, above):
    from_above = [
        jnp.where(subs() == SUBS - 1, above[f], pltpu.roll(up[f], SUBS - 1, 0)) for f in range(5)
    ]
    from_below = [jnp.where(subs() == 0, below[f], pltpu.roll(down[f], 1, 0)) for f in range(5)]
    return from_above, from_below


def along_z(up, down, below, above):
    from_above = [
        jnp.where(lanes() == LANES - 1, above[f], pltpu.roll(up[f], LANES - 1, 1)) for f in range(5)
    ]
    from_below = [jnp.where(lanes() == 0, below[f], pltpu.roll(down[f], 1, 1)) for f in range(5)]
    return from_above, from_below


HALO = 2
ABOVE = 3
FIRST_AT = 33
STRIP_AT = 70
MESSAGE_ROWS = 72


def row_of(u, g, xm, xp, f, row):
    own = g.shape[0] // SUBS
    place = row - HALO
    if place < 0:
        return xm[f * HALO + row]
    if place >= own:
        return xp[f * ABOVE + place - own]
    span = pl.ds(place * SUBS, SUBS)
    return u[f, span, :] if f < 5 else g[span, :]


def strips(load, rows, parts):
    up, down, inner = parts
    for row in rows:
        value = load(row)
        here = lanes() // 2 == row
        up = jnp.where(here, pltpu.roll(value, 2 * row + 2, 1), up)
        down = jnp.where(here, pltpu.roll(value, 2 * row, 1) if row else value, down)
        inner = jnp.where(here, pltpu.roll(value, 2 * row + 1, 1), inner)
    return up, down, inner


def own_strips_kernel(u, g, *parts):
    own = g.shape[0] // SUBS
    for f in range(6):
        result = strips(
            lambda row: row_of(u, g, None, None, f, row),
            range(HALO, HALO + own),
            [jnp.ones((SUBS, LANES), F32)] * 3,
        )
        for part, value in zip(parts, result):
            part[f] = value


def all_strips_kernel(own, xm, xp, own_up, own_down, own_inner, *parts):
    for f in range(6):
        result = (own_up[f], own_down[f], own_inner[f])
        result = strips(lambda row: xm[f * HALO + row], range(HALO), result)
        result = strips(
            lambda row: xp[f * ABOVE + row - HALO - own],
            range(HALO + own, HALO + own + ABOVE),
            result,
        )
        for part, value in zip(parts, result):
            part[f] = value


def strips_of(zm, zp, f):
    odd = lanes() % 2 == 1
    first = jnp.where(odd, zm[f], zp[f])
    second = jnp.where(odd, pltpu.roll(zm[f], 1, 1), pltpu.roll(zp[f], LANES - 1, 1))
    return first, second


def y_kernel(u, g, xm, xp, zm, zp, y_low, y_high):
    own = g.shape[0] // SUBS
    every = own + HALO + ABOVE
    for f in range(6):
        first, _ = strips_of(zm, zp, f)
        for message, near, far in ((y_low, 0, 1), (y_high, SUBS - 1, SUBS - 2)):
            for at, sub, start, stop in (
                (0, far, HALO, HALO + own + 1),
                (FIRST_AT, near, 0, every),
            ):
                for row in range(start, stop):
                    if HALO <= row < HALO + own:
                        continue
                    line = row_of(u, g, xm, xp, f, row)[sub : sub + 1, :]
                    message[f, pl.ds(at + row - start, 1), :] = line
                span = pl.ds(sub, own, stride=SUBS)
                block = u[f, span, :] if f < 5 else g[span, :]
                message[f, pl.ds(at + HALO - start, own), :] = block
            message[f, pl.ds(STRIP_AT, 1), :] = first[near : near + 1, :]
            message[f, pl.ds(STRIP_AT + 1, 1), :] = first[near : near + 1, :]


def sweep(load, first, last, y_below, y_above, z_edge, finish):
    down = down_of(0, load(first - 1))
    pending = None
    for row in range(first, last + 1):
        cell = load(row)
        (x_up, x_down), (y_up, y_down), (z_up, z_down) = halves((0, 1, 2), cell)
        if pending is not None:
            finish(row - 1, [a + b for a, b in zip(pending, x_up)])
        edge = [pltpu.roll(z_edge[f], LANES - 1 - 2 * row, 1) for f in range(5)]
        below = [y_below[f, pl.ds(row, 1), :] for f in range(5)]
        above = [y_above[f, pl.ds(row, 1), :] for f in range(5)]
        core = total_change(
            cell,
            (along_y(y_up, y_down, below, above), along_z(z_up, z_down, edge, edge)),
        )
        pending = [a - b for a, b in zip(core, down)]
        down = x_down
    finish(last, [a + b for a, b in zip(pending, up_of(0, load(last + 1)))])


def lookup(density, species, tables):
    position = (density - density_low) * ((LUT - 1) / (density_high - density_low))
    knot = jnp.clip(jnp.floor(position), 0.0, LUT - 1.0)
    offset = position - knot
    lower_weight = jnp.maximum(0.0, 1.0 - jnp.abs(offset))
    upper_weight = jnp.maximum(0.0, 1.0 - jnp.abs(offset - 1.0))
    index = knot.astype(jnp.int32)
    lane_index = index % LANES
    bits = (index >= LANES, species % 2 == 1, species >= 2)
    result = []
    for channel in range(4):
        total = None
        for side, weight in ((0, lower_weight), (1, upper_weight)):
            values = [
                jnp.take_along_axis(
                    tables[channel, side, k], lane_index, axis=1, mode="promise_in_bounds"
                )
                for k in range(8)
            ]
            for bit in bits:
                values = [
                    jnp.where(bit, values[k + 1], values[k]) for k in range(0, len(values), 2)
                ]
            term = weight * values[0]
            total = term if total is None else total + term
        result.append(total)
    return result


def spread_tables(lut_lower, lut_upper, tables):
    for channel in range(4):
        for k in range(8):
            for side, source in ((0, lut_lower), (1, lut_upper)):
                row = source[pl.ds(channel * 8 + k, 1), :]
                tables[channel, side, k] = jnp.broadcast_to(row, (SUBS, LANES))


def split_dot(value, weights):
    first = value.astype(jnp.bfloat16)
    rest = value - first.astype(F32)
    second = rest.astype(jnp.bfloat16)
    third = (rest - second.astype(F32)).astype(jnp.bfloat16)
    total = jnp.dot(first, weights, preferred_element_type=F32)
    total += jnp.dot(second, weights, preferred_element_type=F32)
    return total + jnp.dot(third, weights, preferred_element_type=F32)


def integrate(properties, grouped, rows):
    extinction = properties[3]
    below = (iota((LANES, LANES), 0) < iota((LANES, LANES), 1)).astype(jnp.bfloat16)
    before = split_dot(extinction, below)
    factor = (1.0 - jnp.exp(-extinction)) * jnp.exp(-before)
    gathered = []
    for channel in range(4):
        if channel < 3:
            weighted = properties[channel] * factor
        else:
            weighted = extinction
        summed = jnp.sum(weighted, axis=1, keepdims=True)
        if channel == 3:
            summed = jnp.exp(-summed)
        plane = jnp.zeros((SUBS, LANES), F32)
        for row in range(rows):
            plane = jnp.where(lanes() == row, summed[row * SUBS : (row + 1) * SUBS], plane)
        gathered.append(plane)
    following = [pltpu.roll(plane, LANES - 1, 1) for plane in gathered]
    block = jnp.concatenate(
        gathered + following + [jnp.zeros((LANES - 8 * SUBS, LANES), F32)], axis=0
    )
    grouped[...] = jnp.transpose(block)[: rows - 1]


def classify(sp, xp, tables, properties, own):
    for place in range(own + 1):
        span = pl.ds(place * SUBS, SUBS)
        kind = sp[span, :] if place < own else xp[6 * ABOVE].astype(jnp.int32)
        found = lookup(properties[0, span, :], kind, tables)
        for channel in range(4):
            properties[channel, span, :] = found[channel]


def step_kernel(
    u, g, sp, xm, xp, zm, zp, z_inner, y_low, y_high, ym, yp, lut_lower, lut_upper,
    grouped, h, y_below2, y_above2, z_edge2, y_below, y_above, z_edge, turned, tables, properties
):
    own = g.shape[0] // SUBS
    spread_tables(lut_lower, lut_upper, tables)
    odd = lanes() % 2 == 1

    for start in (1, 9, 17, 25, 28):
        span = pl.ds(FIRST_AT + start, SUBS)
        below = down_of(1, [ym[f, span, :] for f in range(6)])
        above = up_of(1, [yp[f, span, :] for f in range(6)])
        for f in range(5):
            y_below[f, pl.ds(start, SUBS), :] = below[f]
            y_above[f, pl.ds(start, SUBS), :] = above[f]

    pairs = [strips_of(zm, zp, f) for f in range(6)]
    first = [pair[0] for pair in pairs]
    second = [pair[1] for pair in pairs]
    inner = [z_inner[f] for f in range(6)]
    corner = [
        jnp.where(
            subs() == 0,
            ym[f, pl.ds(STRIP_AT, 1), :],
            jnp.where(subs() == SUBS - 1, yp[f, pl.ds(STRIP_AT, 1), :], 1.0),
        )
        for f in range(6)
    ]
    (corner_up, corner_down), (corner_zup, corner_zdown) = halves((1, 2), corner)
    (x_up, x_down), (y_up, y_down), (z_up, z_down) = halves((0, 1, 2), first)
    for f in range(5):
        z_edge[f] = jnp.where(odd, z_down[f], z_up[f])
    from_above = up_of(2, [jnp.where(odd, a, b) for a, b in zip(inner, second)])
    from_below = down_of(2, [jnp.where(odd, a, b) for a, b in zip(second, inner)])
    change = total_change(
        first,
        (
            (
                [pltpu.roll(q, LANES - 2, 1) for q in x_up],
                [pltpu.roll(q, 2, 1) for q in x_down],
            ),
            along_y(y_up, y_down, corner_down, corner_up),
            (from_above, from_below),
        ),
    )
    halfway = [first[f] - courant * change[f] for f in range(5)] + [first[5]]
    up, down = halves((2,), halfway)[0]
    for f in range(5):
        z_edge2[f] = jnp.where(odd, down[f], up[f])

    ends = [jnp.where(odd, corner_zdown[f], corner_zup[f]) for f in range(5)]
    turned[...] = jnp.transpose(
        jnp.concatenate(ends + [jnp.zeros((LANES - 5 * SUBS, LANES), F32)], axis=0)
    )
    for start in (2, 10, 18, 26, 27):
        z_high_end = turned[pl.ds(2 * start, SUBS, stride=2), :]
        z_low_end = turned[pl.ds(2 * start + 1, SUBS, stride=2), :]
        for message, mine, lower in ((ym, y_low, True), (yp, y_high, False)):
            at = FIRST_AT + start
            cell = [message[f, pl.ds(at, SUBS), :] for f in range(6)]
            x_up = up_of(0, [message[f, pl.ds(at + 1, SUBS), :] for f in range(6)])
            x_down = down_of(0, [message[f, pl.ds(at - 1, SUBS), :] for f in range(6)])
            near = [mine[f, pl.ds(at, SUBS), :] for f in range(6)]
            far = [message[f, pl.ds(start - HALO, SUBS), :] for f in range(6)]
            above, below = (near, far) if lower else (far, near)
            z_up, z_down = halves((2,), cell)[0]
            shift = 0 if lower else SUBS - 1
            low_end = [
                pltpu.roll(z_low_end, (LANES - f * SUBS - shift) % LANES, 1)
                if f * SUBS + shift
                else z_low_end
                for f in range(5)
            ]
            high_end = [
                pltpu.roll(z_high_end, LANES - 1 - f * SUBS - shift, 1) for f in range(5)
            ]
            change = total_change(
                cell,
                (
                    (x_up, x_down),
                    (up_of(1, above), down_of(1, below)),
                    along_z(z_up, z_down, low_end, high_end),
                ),
            )
            halfway = [cell[f] - courant * change[f] for f in range(5)] + [cell[5]]
            part = down_of(1, halfway) if lower else up_of(1, halfway)
            target = y_below2 if lower else y_above2
            for f in range(5):
                target[f, pl.ds(start, SUBS), :] = part[f]

    def at_first(row):
        return [row_of(u, g, xm, xp, f, row) for f in range(6)]

    def store_half(row, change):
        for f in range(5):
            h[f, pl.ds(row * SUBS, SUBS), :] = (
                row_of(u, g, xm, xp, f, row) - courant * change[f]
            )

    sweep(at_first, 1, HALO + own + 1, y_below, y_above, z_edge, store_half)

    def finish(row, change):
        value = 0.5 * (
            row_of(u, g, xm, xp, 0, row) + h[0, pl.ds(row * SUBS, SUBS), :] - courant * change[0]
        )
        properties[0, pl.ds((row - HALO) * SUBS, SUBS), :] = value

    def at_half(row):
        return half_row(h, g, xm, xp, row)

    sweep(at_half, HALO, HALO + own, y_below2, y_above2, z_edge2, finish)
    classify(sp, xp, tables, properties, own)
    integrate(properties, grouped, own + 1)


def half_row(h, g, xm, xp, row):
    return [h[f, pl.ds(row * SUBS, SUBS), :] for f in range(5)] + [
        row_of(None, g, xm, xp, 5, row)
    ]


def state_kernel(u, g, xm, xp, h, y_below2, y_above2, z_edge2, new):
    own = g.shape[0] // SUBS

    def finish(row, change):
        for f in range(5):
            before = row_of(u, g, xm, xp, f, row)
            new[f, pl.ds((row - HALO) * SUBS, SUBS), :] = 0.5 * (
                before + h[f, pl.ds(row * SUBS, SUBS), :] - courant * change[f]
            )

    def at_half(row):
        return half_row(h, g, xm, xp, row)

    sweep(at_half, HALO, HALO + own - 1, y_below2, y_above2, z_edge2, finish)


def image_kernel(across_y, across_z, flags, parts, out):
    lane = iota((across_y, LANES), 1)
    channel = (lane // 8) % 4
    total = None
    for k in reversed(range(across_z)):
        part = parts[pl.ds(k, across_y, stride=across_z), :]
        through = part
        for c in range(3):
            moved = pltpu.roll(part, LANES - (24 - 8 * c), 1)
            through = jnp.where(channel == c, moved, through)
        if total is None:
            total = part
        else:
            total = jnp.where(channel == 3, 0.0, part) + through * total
    total = jnp.where(channel == 3, 1.0 - total, total)
    keep = jnp.where(lane >= 32, flags[0], 1.0)
    total = jnp.where(lane < 64, total * keep, 0.0)
    sub8 = iota((8, LANES), 0)
    lane8 = iota((8, LANES), 1)
    moved = jnp.zeros((8, LANES), F32)
    for k in range(across_y):
        wide = jnp.broadcast_to(total[k : k + 1, :], (8, LANES))
        shifted = wide
        for bit in range(3):
            amount = (LANES - (8 << bit)) % LANES
            shifted = jnp.where(
                (sub8 >> bit) & 1 == 1, pltpu.roll(shifted, amount, 1), shifted
            )
        if k:
            shifted = pltpu.roll(shifted, 8 * k, 1)
        moved = jnp.where(lane8 // 8 == k, shifted, moved)
    columns = 8 * across_y
    moved = jnp.where(lane8 < columns, moved, 0.0)
    screen = jnp.concatenate(
        [
            (1.0 - q / ZOOM) * moved[c : c + 1] + (q / ZOOM) * moved[4 + c : 5 + c]
            for c in range(4)
            for q in range(ZOOM)
        ],
        axis=0,
    )
    zoom = SW // columns
    for tile in range(SW // LANES):
        pixel = iota((8, LANES), 1) + tile * LANES
        source = pixel // zoom
        offset = pixel.astype(F32) * (columns / SW) - source.astype(F32)
        lower = jnp.maximum(0.0, 1.0 - jnp.abs(offset))
        upper = jnp.maximum(0.0, 1.0 - jnp.abs(offset - 1.0))
        for half in range(2):
            block = screen[8 * half : 8 * half + 8]
            value = lower * jnp.take_along_axis(
                block, source, axis=1, mode="promise_in_bounds"
            ) + upper * jnp.take_along_axis(
                block, source + 1, axis=1, mode="promise_in_bounds"
            )
            for c in range(2):
                out[2 * half + c, :, pl.ds(tile * LANES, LANES)] = value[4 * c : 4 * c + 4]


def shifted(value, axis, steps):
    size = lax.axis_size(axis)
    return lax.ppermute(value, axis, [(i, (i + steps) % size) for i in range(size)])


def cost(size):
    return pl.CostEstimate(flops=size, bytes_accessed=size, transcendentals=0)


def struct(*shape):
    return jax.ShapeDtypeStruct(shape, F32)


def local(conserved, gamma_field, species, lut_color, lut_extinction):
    rows = conserved.shape[1]
    cells = rows * SUBS
    params = pltpu.CompilerParams(vmem_limit_bytes=VMEM_LIMIT)
    across_y = lax.axis_size("gy")
    across_z = lax.axis_size("gz")

    lut_table = jnp.concatenate([lut_color, lut_extinction[:, None, :]], axis=1)
    lut_lower = lut_table.transpose(1, 0, 2).reshape(32, LANES)
    lut_upper = (
        jnp.pad(lut_table[:, :, 1:], ((0, 0), (0, 0), (0, 1))).transpose(1, 0, 2).reshape(32, LANES)
    )

    x_low = jnp.concatenate(
        [
            conserved[:, :ABOVE].reshape(5 * ABOVE, SUBS, LANES),
            gamma_field[:ABOVE],
            species[:1].astype(F32),
        ],
        axis=0,
    )
    x_high = jnp.concatenate(
        [conserved[:, rows - HALO :].reshape(5 * HALO, SUBS, LANES), gamma_field[rows - HALO :]],
        axis=0,
    )
    x_low, x_high = lax.optimization_barrier((x_low, x_high))
    xm = shifted(x_high, "gx", 1)
    xp = shifted(x_low, "gx", -1)
    brick = (
        conserved.reshape(5, cells, LANES),
        gamma_field.reshape(cells, LANES),
    )
    strip = struct(6, SUBS, LANES)
    own_parts = pl.pallas_call(
        own_strips_kernel,
        out_shape=(strip, strip, strip),
        compiler_params=params,
        cost_estimate=cost(2_000_000),
        name="own_strips",
    )(*brick)
    z_up, z_down, z_inner = pl.pallas_call(
        functools.partial(all_strips_kernel, rows),
        out_shape=(strip, strip, strip),
        compiler_params=params,
        name="strips",
    )(xm, xp, *own_parts)
    zm = shifted(z_up, "gz", 1)
    zp = shifted(z_down, "gz", -1)
    message = struct(6, MESSAGE_ROWS, LANES)
    y_low, y_high = pl.pallas_call(
        y_kernel, out_shape=(message, message), compiler_params=params, name="layers"
    )(*brick, xm, xp, zm, zp)
    ym = shifted(y_high, "gy", 1)
    yp = shifted(y_low, "gy", -1)
    layer = pltpu.VMEM((5, 40, LANES), F32)
    grouped, *halves_found = pl.pallas_call(
        step_kernel,
        out_shape=(
            struct(rows, LANES),
            struct(5, cells + (HALO + ABOVE) * SUBS, LANES),
            struct(5, 40, LANES),
            struct(5, 40, LANES),
            struct(5, SUBS, LANES),
        ),
        scratch_shapes=[
            layer,
            layer,
            pltpu.VMEM((5, SUBS, LANES), F32),
            pltpu.VMEM((LANES, LANES), F32),
            pltpu.VMEM((4, 2, 8, SUBS, LANES), F32),
            pltpu.VMEM((4, cells + SUBS, LANES), F32),
        ],
        compiler_params=params,
        name="density",
    )(
        *brick,
        species.reshape(cells, LANES),
        xm,
        xp,
        zm,
        zp,
        z_inner,
        y_low,
        y_high,
        ym,
        yp,
        lut_lower,
        lut_upper,
    )
    new_state = pl.pallas_call(
        state_kernel,
        out_shape=struct(5, cells, LANES),
        compiler_params=params,
        cost_estimate=cost(6_000_000),
        name="state",
    )(*brick, xm, xp, *halves_found)
    merged = lax.all_to_all(
        grouped.reshape(across_y * across_z, 1, LANES), ("gy", "gz"), 0, 0, tiled=True
    ).reshape(across_y * across_z, LANES)
    place = lax.axis_index(("gx", "gy", "gz"))
    last = lax.axis_size(("gx", "gy", "gz")) - 1
    flags = jnp.where(place == last, 0.0, 1.0).reshape(1)
    image = pl.pallas_call(
        functools.partial(image_kernel, across_y, across_z),
        out_shape=struct(4, ZOOM, SW),
        in_specs=[
            pl.BlockSpec(memory_space=pltpu.SMEM),
            pl.BlockSpec(memory_space=pltpu.VMEM),
        ],
        compiler_params=params,
        name="image",
    )(flags, merged)
    return new_state.reshape(conserved.shape), image


def solution(mesh):
    return jax.shard_map(
        local,
        mesh=mesh,
        in_specs=(P(None, "gx", "gy", "gz"), P("gx", "gy", "gz"), P("gx", "gy", "gz"), P(), P()),
        out_specs=(P(None, "gx", "gy", "gz"), P(None, ("gx", "gy", "gz"), None)),
        check_vma=False,
    )
```

```python
import functools

import jax
import jax.numpy as jnp
from jax import lax
from jax.experimental import pallas as pl
from jax.experimental.pallas import tpu as pltpu
from jax.sharding import PartitionSpec as P

SW = 1920
ZOOM = 4
CLASSES = 4
LUT = 256
FIXED = 65535

dissipation = 3.0
courant = 0.11
density_low = 0.6
density_high = 1.6

F32 = jnp.float32
LANES = 128
SUBS = 8
VMEM_LIMIT = 48 * 1024 * 1024


def iota(shape, dim):
    return lax.broadcasted_iota(jnp.int32, shape, dim)


def halves(direction, cell):
    density, m1, m2, m3, energy, gamma = cell
    momenta = (m1, m2, m3)
    inverse = 1.0 / density
    kinetic = 0.5 * (m1 * m1 + m2 * m2 + m3 * m3) * inverse
    pressure = (gamma - 1.0) * (energy - kinetic)
    half_p = 0.5 * pressure
    scaled = [(0.5 * dissipation) * q for q in (density, m1, m2, m3, energy)]
    result = []
    for d in direction:
        half_v = 0.5 * momenta[d] * inverse
        flux = [0.5 * momenta[d]]
        for member in range(3):
            component = momenta[member] * half_v
            flux.append(component + half_p if member == d else component)
        flux.append((energy + pressure) * half_v)
        result.append(
            ([a - b for a, b in zip(flux, scaled)], [a + b for a, b in zip(flux, scaled)])
        )
    return result


def up_of(direction, cell):
    return halves((direction,), cell)[0][0]


def down_of(direction, cell):
    return halves((direction,), cell)[0][1]


def total_change(cell, pairs):
    result = []
    for f in range(5):
        total = (6.0 * 0.5 * dissipation) * cell[f]
        for above, below in pairs:
            total = total + (above[f] - below[f])
        result.append(total)
    return result


def lanes():
    return iota((SUBS, LANES), 1)


def subs():
    return iota((SUBS, LANES), 0)


def along_y(up, down, below, above):
    from_above = [
        jnp.where(subs() == SUBS - 1, above[f], pltpu.roll(up[f], SUBS - 1, 0)) for f in range(5)
    ]
    from_below = [jnp.where(subs() == 0, below[f], pltpu.roll(down[f], 1, 0)) for f in range(5)]
    return from_above, from_below


def along_z(up, down, below, above):
    from_above = [
        jnp.where(lanes() == LANES - 1, above[f], pltpu.roll(up[f], LANES - 1, 1)) for f in range(5)
    ]
    from_below = [jnp.where(lanes() == 0, below[f], pltpu.roll(down[f], 1, 1)) for f in range(5)]
    return from_above, from_below


HALO = 2
ABOVE = 3
FIRST_AT = 33
STRIP_AT = 70
MESSAGE_ROWS = 72


def row_of(u, g, xm, xp, f, row):
    own = g.shape[0] // SUBS
    place = row - HALO
    if place < 0:
        return xm[f * HALO + row]
    if place >= own:
        return xp[f * ABOVE + place - own]
    span = pl.ds(place * SUBS, SUBS)
    return u[f, span, :] if f < 5 else g[span, :]


def x_kernel(u, g, sp, x_low, x_high, kinds, semaphores):
    own = u.shape[1]
    moves = []
    for f in range(6):
        source = u.at[f] if f < 5 else g
        moves.append((source.at[pl.ds(0, ABOVE)], x_low.at[pl.ds(f * ABOVE, ABOVE)]))
        moves.append((source.at[pl.ds(own - HALO, HALO)], x_high.at[pl.ds(f * HALO, HALO)]))
    moves.append((sp.at[0], kinds))
    copies = [
        pltpu.make_async_copy(source, target, semaphores.at[k])
        for k, (source, target) in enumerate(moves)
    ]
    for copy in copies:
        copy.start()
    for copy in copies:
        copy.wait()
    x_low[6 * ABOVE] = kinds[...].astype(F32)


def strips(load, rows, parts):
    up, down, inner = parts
    for row in rows:
        value = load(row)
        here = lanes() // 2 == row
        up = jnp.where(here, pltpu.roll(value, 2 * row + 2, 1), up)
        down = jnp.where(here, pltpu.roll(value, 2 * row, 1) if row else value, down)
        inner = jnp.where(here, pltpu.roll(value, 2 * row + 1, 1), inner)
    return up, down, inner


def own_strips_kernel(u, g, *parts):
    own = g.shape[0] // SUBS
    for f in range(6):
        result = strips(
            lambda row: row_of(u, g, None, None, f, row),
            range(HALO, HALO + own),
            [jnp.ones((SUBS, LANES), F32)] * 3,
        )
        for part, value in zip(parts, result):
            part[f] = value


def all_strips_kernel(own, xm, xp, own_up, own_down, own_inner, *parts):
    for f in range(6):
        result = (own_up[f], own_down[f], own_inner[f])
        result = strips(lambda row: xm[f * HALO + row], range(HALO), result)
        result = strips(
            lambda row: xp[f * ABOVE + row - HALO - own],
            range(HALO + own, HALO + own + ABOVE),
            result,
        )
        for part, value in zip(parts, result):
            part[f] = value


def strips_of(zm, zp, f):
    odd = lanes() % 2 == 1
    first = jnp.where(odd, zm[f], zp[f])
    second = jnp.where(odd, pltpu.roll(zm[f], 1, 1), pltpu.roll(zp[f], LANES - 1, 1))
    return first, second


def y_kernel(u, g, xm, xp, zm, zp, y_low, y_high):
    own = g.shape[0] // SUBS
    every = own + HALO + ABOVE
    for f in range(6):
        first, _ = strips_of(zm, zp, f)
        for message, near, far in ((y_low, 0, 1), (y_high, SUBS - 1, SUBS - 2)):
            for at, sub, start, stop in (
                (0, far, HALO, HALO + own + 1),
                (FIRST_AT, near, 0, every),
            ):
                for row in range(start, stop):
                    if HALO <= row < HALO + own:
                        continue
                    line = row_of(u, g, xm, xp, f, row)[sub : sub + 1, :]
                    message[f, pl.ds(at + row - start, 1), :] = line
                span = pl.ds(sub, own, stride=SUBS)
                block = u[f, span, :] if f < 5 else g[span, :]
                message[f, pl.ds(at + HALO - start, own), :] = block
            message[f, pl.ds(STRIP_AT, 1), :] = first[near : near + 1, :]
            message[f, pl.ds(STRIP_AT + 1, 1), :] = first[near : near + 1, :]


def sweep(load, first, last, y_below, y_above, z_edge, finish):
    down = down_of(0, load(first - 1))
    pending = None
    for row in range(first, last + 1):
        cell = load(row)
        (x_up, x_down), (y_up, y_down), (z_up, z_down) = halves((0, 1, 2), cell)
        if pending is not None:
            finish(row - 1, [a + b for a, b in zip(pending, x_up)])
        edge = [pltpu.roll(z_edge[f], LANES - 1 - 2 * row, 1) for f in range(5)]
        if y_below is None:
            below = above = [0.0] * 5
        else:
            below = [y_below[f, pl.ds(row, 1), :] for f in range(5)]
            above = [y_above[f, pl.ds(row, 1), :] for f in range(5)]
        core = total_change(
            cell,
            (along_y(y_up, y_down, below, above), along_z(z_up, z_down, edge, edge)),
        )
        pending = [a - b for a, b in zip(core, down)]
        down = x_down
    finish(last, [a + b for a, b in zip(pending, up_of(0, load(last + 1)))])


def lookup(density, species, colors, extinctions):
    position = (density - density_low) * ((LUT - 1) / (density_high - density_low))
    knot = jnp.clip(jnp.floor(position), 0.0, LUT - 1.0)
    offset = position - knot
    lower_weight = jnp.maximum(0.0, 1.0 - jnp.abs(offset))
    upper_weight = jnp.maximum(0.0, 1.0 - jnp.abs(offset - 1.0))
    index = knot.astype(jnp.int32)
    lane_index = index % LANES
    bits = (index >= LANES, species % 2 == 1, species >= 2)

    def pick(table):
        values = [
            jnp.take_along_axis(table(k), lane_index, axis=1, mode="promise_in_bounds")
            for k in range(8)
        ]
        for bit in bits:
            values = [jnp.where(bit, values[k + 1], values[k]) for k in range(0, len(values), 2)]
        return values[0]

    result = []
    lower_scaled = lower_weight * (1.0 / FIXED)
    upper_scaled = upper_weight * (1.0 / FIXED)
    for channel in range(3):
        both = pick(lambda k: colors[channel, k])
        result.append(
            lower_scaled * (both & FIXED).astype(F32)
            + upper_scaled * lax.shift_right_logical(both, 16).astype(F32)
        )
    result.append(
        lower_weight * pick(lambda k: extinctions[0, k])
        + upper_weight * pick(lambda k: extinctions[1, k])
    )
    return result


def classify(sp, xp, colors, extinctions, properties, own):
    for place in range(own + 1):
        span = pl.ds(place * SUBS, SUBS)
        kind = sp[span, :] if place < own else xp[6 * ABOVE].astype(jnp.int32)
        found = lookup(properties[0, span, :], kind, colors, extinctions)
        for channel in range(4):
            properties[channel, span, :] = found[channel]


def split_dot(value, weights):
    first = value.astype(jnp.bfloat16)
    rest = value - first.astype(F32)
    second = rest.astype(jnp.bfloat16)
    third = (rest - second.astype(F32)).astype(jnp.bfloat16)
    total = jnp.dot(first, weights, preferred_element_type=F32)
    total += jnp.dot(second, weights, preferred_element_type=F32)
    return total + jnp.dot(third, weights, preferred_element_type=F32)


def integrate(properties, grouped, rows, keep):
    extinction = properties[3]
    below = (iota((LANES, LANES), 0) < iota((LANES, LANES), 1)).astype(jnp.bfloat16)
    before = split_dot(extinction, below)
    factor = (1.0 - jnp.exp(-extinction)) * jnp.exp(-before)
    gathered = []
    for channel in range(4):
        if channel < 3:
            weighted = properties[channel] * factor
        else:
            weighted = extinction
        summed = jnp.sum(weighted, axis=1, keepdims=True)
        if channel == 3:
            summed = jnp.exp(-summed)
        plane = jnp.zeros((SUBS, LANES), F32)
        for row in range(rows):
            part = summed[row * SUBS : (row + 1) * SUBS]
            if row == rows - 1:
                part = part * keep + (1.0 - keep if channel == 3 else 0.0)
            plane = jnp.where(lanes() == row, part, plane)
        gathered.append(plane)
    following = [pltpu.roll(plane, LANES - 1, 1) for plane in gathered]
    block = jnp.concatenate(
        gathered + following + [jnp.zeros((LANES - 8 * SUBS, LANES), F32)], axis=0
    )
    grouped[...] = jnp.transpose(block)[: rows - 1]


def half_kernel(u, g, xm, xp, zm, zp, color_rows, extinction_rows, h, colors, extinctions, z_edge):
    own = g.shape[0] // SUBS
    for k in range(24):
        colors[k // 8, k % 8] = jnp.broadcast_to(color_rows[pl.ds(k, 1), :], (SUBS, LANES))
    for k in range(16):
        row = extinction_rows[pl.ds(k, 1), :]
        extinctions[k // 8, k % 8] = jnp.broadcast_to(row, (SUBS, LANES))
    up, down = halves((2,), [strips_of(zm, zp, f)[0] for f in range(6)])[0]
    for f in range(5):
        z_edge[f] = jnp.where(lanes() % 2 == 1, down[f], up[f])

    def at_first(row):
        return [row_of(u, g, xm, xp, f, row) for f in range(6)]

    def store_half(row, change):
        for f in range(5):
            h[f, pl.ds(row * SUBS, SUBS), :] = (
                row_of(u, g, xm, xp, f, row) - courant * change[f]
            )

    sweep(at_first, 1, HALO + own + 1, None, None, z_edge, store_half)


def step_kernel(
    keep, u, g, sp, xm, xp, zm, zp, z_inner, y_low, y_high, ym, yp, partial, colors, extinctions,
    grouped, h, y_below2, y_above2, z_edge2, y_below, y_above, turned, properties
):
    own = g.shape[0] // SUBS
    odd = lanes() % 2 == 1

    for start in (1, 9, 17, 25, 28):
        span = pl.ds(FIRST_AT + start, SUBS)
        below = down_of(1, [ym[f, span, :] for f in range(6)])
        above = up_of(1, [yp[f, span, :] for f in range(6)])
        for f in range(5):
            y_below[f, pl.ds(start, SUBS), :] = courant * below[f]
            y_above[f, pl.ds(start, SUBS), :] = -courant * above[f]

    pairs = [strips_of(zm, zp, f) for f in range(6)]
    first = [pair[0] for pair in pairs]
    second = [pair[1] for pair in pairs]
    inner = [z_inner[f] for f in range(6)]
    corner = [
        jnp.where(
            subs() == 0,
            ym[f, pl.ds(STRIP_AT, 1), :],
            jnp.where(subs() == SUBS - 1, yp[f, pl.ds(STRIP_AT, 1), :], 1.0),
        )
        for f in range(6)
    ]
    (corner_up, corner_down), (corner_zup, corner_zdown) = halves((1, 2), corner)
    (x_up, x_down), (y_up, y_down), (z_up, z_down) = halves((0, 1, 2), first)
    from_above = up_of(2, [jnp.where(odd, a, b) for a, b in zip(inner, second)])
    from_below = down_of(2, [jnp.where(odd, a, b) for a, b in zip(second, inner)])
    change = total_change(
        first,
        (
            (
                [pltpu.roll(q, LANES - 2, 1) for q in x_up],
                [pltpu.roll(q, 2, 1) for q in x_down],
            ),
            along_y(y_up, y_down, corner_down, corner_up),
            (from_above, from_below),
        ),
    )
    halfway = [first[f] - courant * change[f] for f in range(5)] + [first[5]]
    up, down = halves((2,), halfway)[0]
    for f in range(5):
        z_edge2[f] = jnp.where(odd, down[f], up[f])

    ends = [jnp.where(odd, corner_zdown[f], corner_zup[f]) for f in range(5)]
    turned[...] = jnp.transpose(
        jnp.concatenate(ends + [jnp.zeros((LANES - 5 * SUBS, LANES), F32)], axis=0)
    )
    for start in (2, 10, 18, 26, 27):
        z_high_end = turned[pl.ds(2 * start, SUBS, stride=2), :]
        z_low_end = turned[pl.ds(2 * start + 1, SUBS, stride=2), :]
        for message, mine, lower in ((ym, y_low, True), (yp, y_high, False)):
            at = FIRST_AT + start
            cell = [message[f, pl.ds(at, SUBS), :] for f in range(6)]
            x_up = up_of(0, [message[f, pl.ds(at + 1, SUBS), :] for f in range(6)])
            x_down = down_of(0, [message[f, pl.ds(at - 1, SUBS), :] for f in range(6)])
            near = [mine[f, pl.ds(at, SUBS), :] for f in range(6)]
            far = [message[f, pl.ds(start - HALO, SUBS), :] for f in range(6)]
            above, below = (near, far) if lower else (far, near)
            z_up, z_down = halves((2,), cell)[0]
            shift = 0 if lower else SUBS - 1
            low_end = [
                pltpu.roll(z_low_end, (LANES - f * SUBS - shift) % LANES, 1)
                if f * SUBS + shift
                else z_low_end
                for f in range(5)
            ]
            high_end = [
                pltpu.roll(z_high_end, LANES - 1 - f * SUBS - shift, 1) for f in range(5)
            ]
            change = total_change(
                cell,
                (
                    (x_up, x_down),
                    (up_of(1, above), down_of(1, below)),
                    along_z(z_up, z_down, low_end, high_end),
                ),
            )
            halfway = [cell[f] - courant * change[f] for f in range(5)] + [cell[5]]
            part = down_of(1, halfway) if lower else up_of(1, halfway)
            target = y_below2 if lower else y_above2
            for f in range(5):
                target[f, pl.ds(start, SUBS), :] = part[f]

    for row in range(1, HALO + own + 2):
        span = pl.ds(row * SUBS, SUBS)
        for f in range(5):
            low = y_below[f, pl.ds(row, 1), :]
            high = y_above[f, pl.ds(row, 1), :]
            added = jnp.where(subs() == 0, low, jnp.where(subs() == SUBS - 1, high, 0.0))
            h[f, span, :] = partial[f, span, :] + added

    def finish(row, change):
        value = 0.5 * (
            row_of(u, g, xm, xp, 0, row) + h[0, pl.ds(row * SUBS, SUBS), :] - courant * change[0]
        )
        properties[0, pl.ds((row - HALO) * SUBS, SUBS), :] = value

    def at_half(row):
        return half_row(h, g, xm, xp, row)

    sweep(at_half, HALO, HALO + own, y_below2, y_above2, z_edge2, finish)
    classify(sp, xp, colors, extinctions, properties, own)
    integrate(properties, grouped, own + 1, keep[0])


def half_row(h, g, xm, xp, row):
    return [h[f, pl.ds(row * SUBS, SUBS), :] for f in range(5)] + [
        row_of(None, g, xm, xp, 5, row)
    ]


def state_kernel(u, g, xm, xp, h, y_below2, y_above2, z_edge2, new):
    own = g.shape[0] // SUBS

    def finish(row, change):
        for f in range(5):
            before = row_of(u, g, xm, xp, f, row)
            new[f, pl.ds((row - HALO) * SUBS, SUBS), :] = 0.5 * (
                before + h[f, pl.ds(row * SUBS, SUBS), :] - courant * change[f]
            )

    def at_half(row):
        return half_row(h, g, xm, xp, row)

    sweep(at_half, HALO, HALO + own - 1, y_below2, y_above2, z_edge2, finish)


def image_kernel(across_y, across_z, parts, out):
    lane = iota((across_y, LANES), 1)
    channel = (lane // 8) % 4
    total = None
    for k in reversed(range(across_z)):
        part = parts[pl.ds(k, across_y, stride=across_z), :]
        through = part
        for c in range(3):
            moved = pltpu.roll(part, LANES - (24 - 8 * c), 1)
            through = jnp.where(channel == c, moved, through)
        if total is None:
            total = part
        else:
            total = jnp.where(channel == 3, 0.0, part) + through * total
    total = jnp.where(channel == 3, 1.0 - total, total)
    sub8 = iota((8, LANES), 0)
    lane8 = iota((8, LANES), 1)
    moved = jnp.zeros((8, LANES), F32)
    for k in range(across_y):
        wide = jnp.broadcast_to(total[k : k + 1, :], (8, LANES))
        shifted = wide
        for bit in range(3):
            amount = (LANES - (8 << bit)) % LANES
            shifted = jnp.where(
                (sub8 >> bit) & 1 == 1, pltpu.roll(shifted, amount, 1), shifted
            )
        if k:
            shifted = pltpu.roll(shifted, 8 * k, 1)
        moved = jnp.where(lane8 // 8 == k, shifted, moved)
    columns = 8 * across_y
    moved = jnp.where(lane8 < columns, moved, 0.0)
    screen = jnp.concatenate(
        [
            (1.0 - q / ZOOM) * moved[c : c + 1] + (q / ZOOM) * moved[4 + c : 5 + c]
            for c in range(4)
            for q in range(ZOOM)
        ],
        axis=0,
    )
    zoom = SW // columns
    for tile in range(SW // LANES):
        pixel = iota((8, LANES), 1) + tile * LANES
        source = pixel // zoom
        offset = pixel.astype(F32) * (columns / SW) - source.astype(F32)
        lower = jnp.maximum(0.0, 1.0 - jnp.abs(offset))
        upper = jnp.maximum(0.0, 1.0 - jnp.abs(offset - 1.0))
        for half in range(2):
            block = screen[8 * half : 8 * half + 8]
            value = lower * jnp.take_along_axis(
                block, source, axis=1, mode="promise_in_bounds"
            ) + upper * jnp.take_along_axis(
                block, source + 1, axis=1, mode="promise_in_bounds"
            )
            for c in range(2):
                out[2 * half + c, :, pl.ds(tile * LANES, LANES)] = value[4 * c : 4 * c + 4]


def shifted(value, axis, steps):
    size = lax.axis_size(axis)
    return lax.ppermute(value, axis, [(i, (i + steps) % size) for i in range(size)])


def cost(size):
    return pl.CostEstimate(flops=size, bytes_accessed=size, transcendentals=0)


def struct(*shape):
    return jax.ShapeDtypeStruct(shape, F32)


def local(conserved, gamma_field, species, lut_color, lut_extinction):
    rows = conserved.shape[1]
    cells = rows * SUBS
    params = pltpu.CompilerParams(vmem_limit_bytes=VMEM_LIMIT)
    across_y = lax.axis_size("gy")
    across_z = lax.axis_size("gz")

    fixed = jnp.round(jnp.clip(lut_color, 0.0, 1.0) * FIXED).astype(jnp.int32)
    following = jnp.pad(fixed[:, :, 1:], ((0, 0), (0, 0), (0, 1)))
    color_rows = (fixed + lax.shift_left(following, 16)).transpose(1, 0, 2).reshape(24, LANES)
    extinction_rows = jnp.stack(
        [lut_extinction, jnp.pad(lut_extinction[:, 1:], ((0, 0), (0, 1)))]
    ).reshape(16, LANES)

    in_hbm = pl.BlockSpec(memory_space=pltpu.HBM)
    x_low, x_high = pl.pallas_call(
        x_kernel,
        out_shape=(struct(6 * ABOVE + 1, SUBS, LANES), struct(6 * HALO, SUBS, LANES)),
        in_specs=[in_hbm, in_hbm, in_hbm],
        scratch_shapes=[pltpu.VMEM((SUBS, LANES), jnp.int32), pltpu.SemaphoreType.DMA((13,))],
        compiler_params=pltpu.CompilerParams(vmem_limit_bytes=60 * 1024 * 1024),
        name="x_layers",
    )(conserved, gamma_field, species)
    xm = shifted(x_high, "gx", 1)
    xp = shifted(x_low, "gx", -1)
    brick = (
        conserved.reshape(5, cells, LANES),
        gamma_field.reshape(cells, LANES),
    )
    strip = struct(6, SUBS, LANES)
    own_parts = pl.pallas_call(
        own_strips_kernel,
        out_shape=(strip, strip, strip),
        compiler_params=params,
        cost_estimate=cost(2_000_000),
        name="own_strips",
    )(*brick)
    z_up, z_down, z_inner = pl.pallas_call(
        functools.partial(all_strips_kernel, rows),
        out_shape=(strip, strip, strip),
        compiler_params=params,
        name="strips",
    )(xm, xp, *own_parts)
    zm = shifted(z_up, "gz", 1)
    zp = shifted(z_down, "gz", -1)
    message = struct(6, MESSAGE_ROWS, LANES)
    y_low, y_high = pl.pallas_call(
        y_kernel, out_shape=(message, message), compiler_params=params, name="layers"
    )(*brick, xm, xp, zm, zp)
    ym = shifted(y_high, "gy", 1)
    yp = shifted(y_low, "gy", -1)
    every = cells + (HALO + ABOVE) * SUBS
    partial, colors, extinctions = pl.pallas_call(
        half_kernel,
        out_shape=(
            struct(5, every, LANES),
            jax.ShapeDtypeStruct((3, 8, SUBS, LANES), jnp.int32),
            struct(2, 8, SUBS, LANES),
        ),
        scratch_shapes=[pltpu.VMEM((5, SUBS, LANES), F32)],
        compiler_params=params,
        cost_estimate=cost(4_000_000),
        name="half",
    )(*brick, xm, xp, zm, zp, color_rows, extinction_rows)
    layer = pltpu.VMEM((5, 40, LANES), F32)
    place = lax.axis_index("gx")
    keep = jnp.where(place == lax.axis_size("gx") - 1, 0.0, 1.0).reshape(1)
    vmem = pl.BlockSpec(memory_space=pltpu.VMEM)
    grouped, *halves_found = pl.pallas_call(
        step_kernel,
        in_specs=[pl.BlockSpec(memory_space=pltpu.SMEM)] + [vmem] * 15,
        out_shape=(
            struct(rows, LANES),
            struct(5, every, LANES),
            struct(5, 40, LANES),
            struct(5, 40, LANES),
            struct(5, SUBS, LANES),
        ),
        scratch_shapes=[
            layer,
            layer,
            pltpu.VMEM((LANES, LANES), F32),
            pltpu.VMEM((4, cells + SUBS, LANES), F32),
        ],
        compiler_params=params,
        name="density",
    )(
        keep,
        *brick,
        species.reshape(cells, LANES),
        xm,
        xp,
        zm,
        zp,
        z_inner,
        y_low,
        y_high,
        ym,
        yp,
        partial,
        colors,
        extinctions,
    )
    new_state = pl.pallas_call(
        state_kernel,
        out_shape=struct(5, cells, LANES),
        compiler_params=params,
        cost_estimate=cost(6_000_000),
        name="state",
    )(*brick, xm, xp, *halves_found)
    merged = lax.all_to_all(
        grouped.reshape(across_y * across_z, 1, LANES), ("gy", "gz"), 0, 0, tiled=True
    ).reshape(across_y * across_z, LANES)
    image = pl.pallas_call(
        functools.partial(image_kernel, across_y, across_z),
        out_shape=struct(4, ZOOM, SW),
        compiler_params=params,
        name="image",
    )(merged)
    return new_state.reshape(conserved.shape), image


def solution(mesh):
    return jax.shard_map(
        local,
        mesh=mesh,
        in_specs=(P(None, "gx", "gy", "gz"), P("gx", "gy", "gz"), P("gx", "gy", "gz"), P(), P()),
        out_specs=(P(None, "gx", "gy", "gz"), P(None, ("gx", "gy", "gz"), None)),
        check_vma=False,
    )
```

```python
import functools

import jax
import jax.numpy as jnp
from jax import lax
from jax.experimental import pallas as pl
from jax.experimental.pallas import tpu as pltpu
from jax.sharding import PartitionSpec as P

SW = 1920
ZOOM = 4
CLASSES = 4
LUT = 256
FIXED = 65535
EXTINCTION_TOP = 0.01

dissipation = 3.0
courant = 0.11
density_low = 0.6
density_high = 1.6

F32 = jnp.float32
LANES = 128
SUBS = 8
VMEM_LIMIT = 48 * 1024 * 1024


def iota(shape, dim):
    return lax.broadcasted_iota(jnp.int32, shape, dim)


def halves(direction, cell):
    density, m1, m2, m3, energy, gamma = cell
    momenta = (m1, m2, m3)
    inverse = 1.0 / density
    kinetic = 0.5 * (m1 * m1 + m2 * m2 + m3 * m3) * inverse
    pressure = (gamma - 1.0) * (energy - kinetic)
    half_p = 0.5 * pressure
    scaled = [(0.5 * dissipation) * q for q in (density, m1, m2, m3, energy)]
    result = []
    for d in direction:
        half_v = 0.5 * momenta[d] * inverse
        flux = [0.5 * momenta[d]]
        for member in range(3):
            component = momenta[member] * half_v
            flux.append(component + half_p if member == d else component)
        flux.append((energy + pressure) * half_v)
        result.append(
            ([a - b for a, b in zip(flux, scaled)], [a + b for a, b in zip(flux, scaled)])
        )
    return result


def up_of(direction, cell):
    return halves((direction,), cell)[0][0]


def down_of(direction, cell):
    return halves((direction,), cell)[0][1]


def total_change(cell, pairs):
    result = []
    for f in range(5):
        total = (6.0 * 0.5 * dissipation) * cell[f]
        for above, below in pairs:
            total = total + (above[f] - below[f])
        result.append(total)
    return result


def lanes():
    return iota((SUBS, LANES), 1)


def subs():
    return iota((SUBS, LANES), 0)


def along_y(up, down, below, above):
    from_above = [
        jnp.where(subs() == SUBS - 1, above[f], pltpu.roll(up[f], SUBS - 1, 0)) for f in range(5)
    ]
    from_below = [jnp.where(subs() == 0, below[f], pltpu.roll(down[f], 1, 0)) for f in range(5)]
    return from_above, from_below


def along_z(up, down, below, above):
    from_above = [
        jnp.where(lanes() == LANES - 1, above[f], pltpu.roll(up[f], LANES - 1, 1)) for f in range(5)
    ]
    from_below = [jnp.where(lanes() == 0, below[f], pltpu.roll(down[f], 1, 1)) for f in range(5)]
    return from_above, from_below


HALO = 2
ABOVE = 3
FIRST_AT = 33
STRIP_AT = 70
MESSAGE_ROWS = 72


def row_of(u, g, xm, xp, f, row):
    own = g.shape[0] // SUBS
    place = row - HALO
    if place < 0:
        return xm[f * HALO + row]
    if place >= own:
        return xp[f * ABOVE + place - own]
    span = pl.ds(place * SUBS, SUBS)
    return u[f, span, :] if f < 5 else g[span, :]


def x_kernel(u, g, sp, x_low, x_high, kinds, semaphores):
    own = u.shape[1]
    moves = []
    for f in range(6):
        source = u.at[f] if f < 5 else g
        moves.append((source.at[pl.ds(0, ABOVE)], x_low.at[pl.ds(f * ABOVE, ABOVE)]))
        moves.append((source.at[pl.ds(own - HALO, HALO)], x_high.at[pl.ds(f * HALO, HALO)]))
    moves.append((sp.at[0], kinds))
    copies = [
        pltpu.make_async_copy(source, target, semaphores.at[k])
        for k, (source, target) in enumerate(moves)
    ]
    for copy in copies:
        copy.start()
    for copy in copies:
        copy.wait()
    x_low[6 * ABOVE] = kinds[...].astype(F32)


def strips(load, rows, parts):
    up, down, inner = parts
    for row in rows:
        value = load(row)
        here = lanes() // 2 == row
        up = jnp.where(here, pltpu.roll(value, 2 * row + 2, 1), up)
        down = jnp.where(here, pltpu.roll(value, 2 * row, 1) if row else value, down)
        inner = jnp.where(here, pltpu.roll(value, 2 * row + 1, 1), inner)
    return up, down, inner


def own_strips_kernel(u, g, *parts):
    own = g.shape[0] // SUBS
    for f in range(6):
        result = strips(
            lambda row: row_of(u, g, None, None, f, row),
            range(HALO, HALO + own),
            [jnp.ones((SUBS, LANES), F32)] * 3,
        )
        for part, value in zip(parts, result):
            part[f] = value


def all_strips_kernel(own, xm, xp, own_up, own_down, own_inner, *parts):
    for f in range(6):
        result = (own_up[f], own_down[f], own_inner[f])
        result = strips(lambda row: xm[f * HALO + row], range(HALO), result)
        result = strips(
            lambda row: xp[f * ABOVE + row - HALO - own],
            range(HALO + own, HALO + own + ABOVE),
            result,
        )
        for part, value in zip(parts, result):
            part[f] = value


def strips_of(zm, zp, f):
    odd = lanes() % 2 == 1
    first = jnp.where(odd, zm[f], zp[f])
    second = jnp.where(odd, pltpu.roll(zm[f], 1, 1), pltpu.roll(zp[f], LANES - 1, 1))
    return first, second


def y_kernel(u, g, xm, xp, zm, zp, y_low, y_high):
    own = g.shape[0] // SUBS
    every = own + HALO + ABOVE
    for f in range(6):
        first, _ = strips_of(zm, zp, f)
        for message, near, far in ((y_low, 0, 1), (y_high, SUBS - 1, SUBS - 2)):
            for at, sub, start, stop in (
                (0, far, HALO, HALO + own + 1),
                (FIRST_AT, near, 0, every),
            ):
                for row in range(start, stop):
                    if HALO <= row < HALO + own:
                        continue
                    line = row_of(u, g, xm, xp, f, row)[sub : sub + 1, :]
                    message[f, pl.ds(at + row - start, 1), :] = line
                span = pl.ds(sub, own, stride=SUBS)
                block = u[f, span, :] if f < 5 else g[span, :]
                message[f, pl.ds(at + HALO - start, own), :] = block
            message[f, pl.ds(STRIP_AT, 1), :] = first[near : near + 1, :]
            message[f, pl.ds(STRIP_AT + 1, 1), :] = first[near : near + 1, :]


def sweep(load, first, last, y_below, y_above, z_edge, finish):
    down = down_of(0, load(first - 1))
    pending = None
    for row in range(first, last + 1):
        cell = load(row)
        (x_up, x_down), (y_up, y_down), (z_up, z_down) = halves((0, 1, 2), cell)
        if pending is not None:
            finish(row - 1, [a + b for a, b in zip(pending, x_up)])
        edge = [pltpu.roll(z_edge[f], LANES - 1 - 2 * row, 1) for f in range(5)]
        if y_below is None:
            below = above = [0.0] * 5
        else:
            below = [y_below[f, pl.ds(row, 1), :] for f in range(5)]
            above = [y_above[f, pl.ds(row, 1), :] for f in range(5)]
        core = total_change(
            cell,
            (along_y(y_up, y_down, below, above), along_z(z_up, z_down, edge, edge)),
        )
        pending = [a - b for a, b in zip(core, down)]
        down = x_down
    finish(last, [a + b for a, b in zip(pending, up_of(0, load(last + 1)))])


def lookup(density, species, tables):
    position = (density - density_low) * ((LUT - 1) / (density_high - density_low))
    knot = jnp.clip(jnp.floor(position), 0.0, LUT - 1.0)
    offset = position - knot
    lower_weight = jnp.maximum(0.0, 1.0 - jnp.abs(offset))
    upper_weight = jnp.maximum(0.0, 1.0 - jnp.abs(offset - 1.0))
    index = knot.astype(jnp.int32)
    lane_index = index % LANES
    bits = (index >= LANES, species % 2 == 1, species >= 2)

    def pick(table):
        values = [
            jnp.take_along_axis(table(k), lane_index, axis=1, mode="promise_in_bounds")
            for k in range(8)
        ]
        for bit in bits:
            values = [jnp.where(bit, values[k + 1], values[k]) for k in range(0, len(values), 2)]
        return values[0]

    def knots(channel):
        both = pick(lambda k: tables[channel, k])
        return (both & FIXED).astype(F32), lax.shift_right_logical(both, 16).astype(F32)

    result = []
    lower_scaled = lower_weight * (1.0 / FIXED)
    upper_scaled = upper_weight * (1.0 / FIXED)
    for channel in range(3):
        lower, upper = knots(channel)
        result.append(lower_scaled * lower + upper_scaled * upper)
    lower, upper = knots(3)
    scale = EXTINCTION_TOP / (FIXED * FIXED)
    result.append(
        (lower_weight * scale) * (lower * lower) + (upper_weight * scale) * (upper * upper)
    )
    return result


def classify(sp, xp, tables, properties, own):
    for place in range(own + 1):
        span = pl.ds(place * SUBS, SUBS)
        kind = sp[span, :] if place < own else xp[6 * ABOVE].astype(jnp.int32)
        found = lookup(properties[0, span, :], kind, tables)
        for channel in range(4):
            properties[channel, span, :] = found[channel]


def split_dot(value, weights):
    first = value.astype(jnp.bfloat16)
    rest = value - first.astype(F32)
    second = rest.astype(jnp.bfloat16)
    third = (rest - second.astype(F32)).astype(jnp.bfloat16)
    total = jnp.dot(first, weights, preferred_element_type=F32)
    total += jnp.dot(second, weights, preferred_element_type=F32)
    return total + jnp.dot(third, weights, preferred_element_type=F32)


def integrate(properties, grouped, rows, keep):
    extinction = properties[3]
    below = (iota((LANES, LANES), 0) < iota((LANES, LANES), 1)).astype(jnp.bfloat16)
    before = split_dot(extinction, below)
    factor = (1.0 - jnp.exp(-extinction)) * jnp.exp(-before)
    gathered = []
    for channel in range(4):
        if channel < 3:
            weighted = properties[channel] * factor
        else:
            weighted = extinction
        summed = jnp.sum(weighted, axis=1, keepdims=True)
        if channel == 3:
            summed = jnp.exp(-summed)
        plane = jnp.zeros((SUBS, LANES), F32)
        for row in range(rows):
            part = summed[row * SUBS : (row + 1) * SUBS]
            if row == rows - 1:
                part = part * keep + (1.0 - keep if channel == 3 else 0.0)
            plane = jnp.where(lanes() == row, part, plane)
        gathered.append(plane)
    following = [pltpu.roll(plane, LANES - 1, 1) for plane in gathered]
    block = jnp.concatenate(
        gathered + following + [jnp.zeros((LANES - 8 * SUBS, LANES), F32)], axis=0
    )
    grouped[...] = jnp.transpose(block)[: rows - 1]


def half_kernel(u, g, xm, xp, zm, zp, table_rows, h, tables, z_edge):
    own = g.shape[0] // SUBS
    for k in range(32):
        tables[k // 8, k % 8] = jnp.broadcast_to(table_rows[pl.ds(k, 1), :], (SUBS, LANES))
    up, down = halves((2,), [strips_of(zm, zp, f)[0] for f in range(6)])[0]
    for f in range(5):
        z_edge[f] = jnp.where(lanes() % 2 == 1, down[f], up[f])

    def at_first(row):
        return [row_of(u, g, xm, xp, f, row) for f in range(6)]

    def store_half(row, change):
        for f in range(5):
            h[f, pl.ds(row * SUBS, SUBS), :] = (
                row_of(u, g, xm, xp, f, row) - courant * change[f]
            )

    sweep(at_first, 1, HALO + own + 1, None, None, z_edge, store_half)


def step_kernel(
    keep, u, g, sp, xm, xp, zm, zp, z_inner, y_low, y_high, ym, yp, partial, tables,
    grouped, h, y_below2, y_above2, z_edge2, y_below, y_above, turned, properties
):
    own = g.shape[0] // SUBS
    odd = lanes() % 2 == 1

    for start in (1, 9, 17, 25, 28):
        span = pl.ds(FIRST_AT + start, SUBS)
        below = down_of(1, [ym[f, span, :] for f in range(6)])
        above = up_of(1, [yp[f, span, :] for f in range(6)])
        for f in range(5):
            y_below[f, pl.ds(start, SUBS), :] = courant * below[f]
            y_above[f, pl.ds(start, SUBS), :] = -courant * above[f]

    pairs = [strips_of(zm, zp, f) for f in range(6)]
    first = [pair[0] for pair in pairs]
    second = [pair[1] for pair in pairs]
    inner = [z_inner[f] for f in range(6)]
    corner = [
        jnp.where(
            subs() == 0,
            ym[f, pl.ds(STRIP_AT, 1), :],
            jnp.where(subs() == SUBS - 1, yp[f, pl.ds(STRIP_AT, 1), :], 1.0),
        )
        for f in range(6)
    ]
    (corner_up, corner_down), (corner_zup, corner_zdown) = halves((1, 2), corner)
    (x_up, x_down), (y_up, y_down), (z_up, z_down) = halves((0, 1, 2), first)
    from_above = up_of(2, [jnp.where(odd, a, b) for a, b in zip(inner, second)])
    from_below = down_of(2, [jnp.where(odd, a, b) for a, b in zip(second, inner)])
    change = total_change(
        first,
        (
            (
                [pltpu.roll(q, LANES - 2, 1) for q in x_up],
                [pltpu.roll(q, 2, 1) for q in x_down],
            ),
            along_y(y_up, y_down, corner_down, corner_up),
            (from_above, from_below),
        ),
    )
    halfway = [first[f] - courant * change[f] for f in range(5)] + [first[5]]
    up, down = halves((2,), halfway)[0]
    for f in range(5):
        z_edge2[f] = jnp.where(odd, down[f], up[f])

    ends = [jnp.where(odd, corner_zdown[f], corner_zup[f]) for f in range(5)]
    turned[...] = jnp.transpose(
        jnp.concatenate(ends + [jnp.zeros((LANES - 5 * SUBS, LANES), F32)], axis=0)
    )
    for start in (2, 10, 18, 26, 27):
        z_high_end = turned[pl.ds(2 * start, SUBS, stride=2), :]
        z_low_end = turned[pl.ds(2 * start + 1, SUBS, stride=2), :]
        for message, mine, lower in ((ym, y_low, True), (yp, y_high, False)):
            at = FIRST_AT + start
            cell = [message[f, pl.ds(at, SUBS), :] for f in range(6)]
            x_up = up_of(0, [message[f, pl.ds(at + 1, SUBS), :] for f in range(6)])
            x_down = down_of(0, [message[f, pl.ds(at - 1, SUBS), :] for f in range(6)])
            near = [mine[f, pl.ds(at, SUBS), :] for f in range(6)]
            far = [message[f, pl.ds(start - HALO, SUBS), :] for f in range(6)]
            above, below = (near, far) if lower else (far, near)
            z_up, z_down = halves((2,), cell)[0]
            shift = 0 if lower else SUBS - 1
            low_end = [
                pltpu.roll(z_low_end, (LANES - f * SUBS - shift) % LANES, 1)
                if f * SUBS + shift
                else z_low_end
                for f in range(5)
            ]
            high_end = [
                pltpu.roll(z_high_end, LANES - 1 - f * SUBS - shift, 1) for f in range(5)
            ]
            change = total_change(
                cell,
                (
                    (x_up, x_down),
                    (up_of(1, above), down_of(1, below)),
                    along_z(z_up, z_down, low_end, high_end),
                ),
            )
            halfway = [cell[f] - courant * change[f] for f in range(5)] + [cell[5]]
            part = down_of(1, halfway) if lower else up_of(1, halfway)
            target = y_below2 if lower else y_above2
            for f in range(5):
                target[f, pl.ds(start, SUBS), :] = part[f]

    for row in range(1, HALO + own + 2):
        span = pl.ds(row * SUBS, SUBS)
        for f in range(5):
            low = y_below[f, pl.ds(row, 1), :]
            high = y_above[f, pl.ds(row, 1), :]
            added = jnp.where(subs() == 0, low, jnp.where(subs() == SUBS - 1, high, 0.0))
            h[f, span, :] = partial[f, span, :] + added

    def finish(row, change):
        value = 0.5 * (
            row_of(u, g, xm, xp, 0, row) + h[0, pl.ds(row * SUBS, SUBS), :] - courant * change[0]
        )
        properties[0, pl.ds((row - HALO) * SUBS, SUBS), :] = value

    def at_half(row):
        return half_row(h, g, xm, xp, row)

    sweep(at_half, HALO, HALO + own, y_below2, y_above2, z_edge2, finish)
    classify(sp, xp, tables, properties, own)
    integrate(properties, grouped, own + 1, keep[0])


def half_row(h, g, xm, xp, row):
    return [h[f, pl.ds(row * SUBS, SUBS), :] for f in range(5)] + [
        row_of(None, g, xm, xp, 5, row)
    ]


def state_kernel(u, g, xm, xp, h, y_below2, y_above2, z_edge2, new):
    own = g.shape[0] // SUBS

    def finish(row, change):
        for f in range(5):
            before = row_of(u, g, xm, xp, f, row)
            new[f, pl.ds((row - HALO) * SUBS, SUBS), :] = 0.5 * (
                before + h[f, pl.ds(row * SUBS, SUBS), :] - courant * change[f]
            )

    def at_half(row):
        return half_row(h, g, xm, xp, row)

    sweep(at_half, HALO, HALO + own - 1, y_below2, y_above2, z_edge2, finish)


def image_kernel(across_y, across_z, parts, out):
    lane = iota((across_y, LANES), 1)
    channel = (lane // 8) % 4
    total = None
    for k in reversed(range(across_z)):
        part = parts[pl.ds(k, across_y, stride=across_z), :]
        through = part
        for c in range(3):
            moved = pltpu.roll(part, LANES - (24 - 8 * c), 1)
            through = jnp.where(channel == c, moved, through)
        if total is None:
            total = part
        else:
            total = jnp.where(channel == 3, 0.0, part) + through * total
    total = jnp.where(channel == 3, 1.0 - total, total)
    sub8 = iota((8, LANES), 0)
    lane8 = iota((8, LANES), 1)
    moved = jnp.zeros((8, LANES), F32)
    for k in range(across_y):
        wide = jnp.broadcast_to(total[k : k + 1, :], (8, LANES))
        shifted = wide
        for bit in range(3):
            amount = (LANES - (8 << bit)) % LANES
            shifted = jnp.where(
                (sub8 >> bit) & 1 == 1, pltpu.roll(shifted, amount, 1), shifted
            )
        if k:
            shifted = pltpu.roll(shifted, 8 * k, 1)
        moved = jnp.where(lane8 // 8 == k, shifted, moved)
    columns = 8 * across_y
    moved = jnp.where(lane8 < columns, moved, 0.0)
    screen = jnp.concatenate(
        [
            (1.0 - q / ZOOM) * moved[c : c + 1] + (q / ZOOM) * moved[4 + c : 5 + c]
            for c in range(4)
            for q in range(ZOOM)
        ],
        axis=0,
    )
    zoom = SW // columns
    for tile in range(SW // LANES):
        pixel = iota((8, LANES), 1) + tile * LANES
        whole = jnp.floor((pixel.astype(F32) + 0.5) * (1.0 / zoom))
        source = whole.astype(jnp.int32)
        offset = pixel.astype(F32) * (columns / SW) - whole
        lower = jnp.maximum(0.0, 1.0 - jnp.abs(offset))
        upper = jnp.maximum(0.0, 1.0 - jnp.abs(offset - 1.0))
        for half in range(2):
            block = screen[8 * half : 8 * half + 8]
            value = lower * jnp.take_along_axis(
                block, source, axis=1, mode="promise_in_bounds"
            ) + upper * jnp.take_along_axis(
                block, source + 1, axis=1, mode="promise_in_bounds"
            )
            for c in range(2):
                out[2 * half + c, :, pl.ds(tile * LANES, LANES)] = value[4 * c : 4 * c + 4]


def shifted(value, axis, steps):
    size = lax.axis_size(axis)
    return lax.ppermute(value, axis, [(i, (i + steps) % size) for i in range(size)])


def cost(size):
    return pl.CostEstimate(flops=size, bytes_accessed=size, transcendentals=0)


def struct(*shape):
    return jax.ShapeDtypeStruct(shape, F32)


def local(conserved, gamma_field, species, lut_color, lut_extinction):
    rows = conserved.shape[1]
    cells = rows * SUBS
    params = pltpu.CompilerParams(vmem_limit_bytes=VMEM_LIMIT)
    across_y = lax.axis_size("gy")
    across_z = lax.axis_size("gz")

    roots = jnp.sqrt(jnp.clip(lut_extinction, 0.0, EXTINCTION_TOP) * (1.0 / EXTINCTION_TOP))
    values = jnp.concatenate([jnp.clip(lut_color, 0.0, 1.0), roots[:, None, :]], axis=1)
    fixed = jnp.round(values * FIXED).astype(jnp.int32)
    following = jnp.pad(fixed[:, :, 1:], ((0, 0), (0, 0), (0, 1)))
    table_rows = (fixed + lax.shift_left(following, 16)).transpose(1, 0, 2).reshape(32, LANES)

    in_hbm = pl.BlockSpec(memory_space=pltpu.HBM)
    x_low, x_high = pl.pallas_call(
        x_kernel,
        out_shape=(struct(6 * ABOVE + 1, SUBS, LANES), struct(6 * HALO, SUBS, LANES)),
        in_specs=[in_hbm, in_hbm, in_hbm],
        scratch_shapes=[pltpu.VMEM((SUBS, LANES), jnp.int32), pltpu.SemaphoreType.DMA((13,))],
        compiler_params=pltpu.CompilerParams(vmem_limit_bytes=VMEM_LIMIT),
        name="x_layers",
    )(*[pltpu.with_memory_space_constraint(q, pltpu.HBM) for q in (conserved, gamma_field, species)])
    x_low, x_high, conserved, gamma_field = lax.optimization_barrier(
        (x_low, x_high, conserved, gamma_field)
    )
    xm = shifted(x_high, "gx", 1)
    xp = shifted(x_low, "gx", -1)
    brick = (
        conserved.reshape(5, cells, LANES),
        gamma_field.reshape(cells, LANES),
    )
    strip = struct(6, SUBS, LANES)
    own_parts = pl.pallas_call(
        own_strips_kernel,
        out_shape=(strip, strip, strip),
        compiler_params=params,
        cost_estimate=cost(2_000_000),
        name="own_strips",
    )(*brick)
    z_up, z_down, z_inner = pl.pallas_call(
        functools.partial(all_strips_kernel, rows),
        out_shape=(strip, strip, strip),
        compiler_params=params,
        name="strips",
    )(xm, xp, *own_parts)
    zm = shifted(z_up, "gz", 1)
    zp = shifted(z_down, "gz", -1)
    message = struct(6, MESSAGE_ROWS, LANES)
    y_low, y_high = pl.pallas_call(
        y_kernel, out_shape=(message, message), compiler_params=params, name="layers"
    )(*brick, xm, xp, zm, zp)
    ym = shifted(y_high, "gy", 1)
    yp = shifted(y_low, "gy", -1)
    every = cells + (HALO + ABOVE) * SUBS
    partial, tables = pl.pallas_call(
        half_kernel,
        out_shape=(
            struct(5, every, LANES),
            jax.ShapeDtypeStruct((4, 8, SUBS, LANES), jnp.int32),
        ),
        scratch_shapes=[pltpu.VMEM((5, SUBS, LANES), F32)],
        compiler_params=params,
        cost_estimate=cost(4_000_000),
        name="half",
    )(*brick, xm, xp, zm, zp, table_rows)
    layer = pltpu.VMEM((5, 40, LANES), F32)
    place = lax.axis_index("gx")
    keep = jnp.where(place == lax.axis_size("gx") - 1, 0.0, 1.0).reshape(1)
    vmem = pl.BlockSpec(memory_space=pltpu.VMEM)
    grouped, *halves_found = pl.pallas_call(
        step_kernel,
        in_specs=[pl.BlockSpec(memory_space=pltpu.SMEM)] + [vmem] * 14,
        out_shape=(
            struct(rows, LANES),
            struct(5, every, LANES),
            struct(5, 40, LANES),
            struct(5, 40, LANES),
            struct(5, SUBS, LANES),
        ),
        scratch_shapes=[
            layer,
            layer,
            pltpu.VMEM((LANES, LANES), F32),
            pltpu.VMEM((4, cells + SUBS, LANES), F32),
        ],
        compiler_params=params,
        name="density",
    )(
        keep,
        *brick,
        species.reshape(cells, LANES),
        xm,
        xp,
        zm,
        zp,
        z_inner,
        y_low,
        y_high,
        ym,
        yp,
        partial,
        tables,
    )
    new_state = pl.pallas_call(
        state_kernel,
        out_shape=struct(5, cells, LANES),
        compiler_params=params,
        cost_estimate=cost(6_000_000),
        name="state",
    )(*brick, xm, xp, *halves_found)
    merged = lax.all_to_all(
        grouped.reshape(across_y * across_z, 1, LANES), ("gy", "gz"), 0, 0, tiled=True
    ).reshape(across_y * across_z, LANES)
    image = pl.pallas_call(
        functools.partial(image_kernel, across_y, across_z),
        out_shape=struct(4, ZOOM, SW),
        compiler_params=params,
        name="image",
    )(merged)
    return new_state.reshape(conserved.shape), image


def solution(mesh):
    return jax.shard_map(
        local,
        mesh=mesh,
        in_specs=(P(None, "gx", "gy", "gz"), P("gx", "gy", "gz"), P("gx", "gy", "gz"), P(), P()),
        out_specs=(P(None, "gx", "gy", "gz"), P(None, ("gx", "gy", "gz"), None)),
        check_vma=False,
    )
```

```python
import functools

import jax
import jax.numpy as jnp
from jax import lax
from jax.experimental import pallas as pl
from jax.experimental.pallas import tpu as pltpu
from jax.sharding import PartitionSpec as P

SW = 1920
ZOOM = 4
CLASSES = 4
LUT = 256
FIXED = 65535
EXTINCTION_TOP = 0.01

dissipation = 3.0
courant = 0.11
density_low = 0.6
density_high = 1.6

F32 = jnp.float32
LANES = 128
SUBS = 8
VMEM_LIMIT = 51 * 1024 * 1024


def iota(shape, dim):
    return lax.broadcasted_iota(jnp.int32, shape, dim)


def halves(direction, cell):
    density, m1, m2, m3, energy, gamma = cell
    momenta = (m1, m2, m3)
    inverse = 1.0 / density
    kinetic = 0.5 * (m1 * m1 + m2 * m2 + m3 * m3) * inverse
    pressure = (gamma - 1.0) * (energy - kinetic)
    half_p = 0.5 * pressure
    scaled = [(0.5 * dissipation) * q for q in (density, m1, m2, m3, energy)]
    result = []
    for d in direction:
        half_v = 0.5 * momenta[d] * inverse
        flux = [0.5 * momenta[d]]
        for member in range(3):
            component = momenta[member] * half_v
            flux.append(component + half_p if member == d else component)
        flux.append((energy + pressure) * half_v)
        result.append(
            ([a - b for a, b in zip(flux, scaled)], [a + b for a, b in zip(flux, scaled)])
        )
    return result


def up_of(direction, cell):
    return halves((direction,), cell)[0][0]


def down_of(direction, cell):
    return halves((direction,), cell)[0][1]


def total_change(cell, pairs):
    result = []
    for f in range(5):
        total = (6.0 * 0.5 * dissipation) * cell[f]
        for above, below in pairs:
            total = total + (above[f] - below[f])
        result.append(total)
    return result


def lanes():
    return iota((SUBS, LANES), 1)


def subs():
    return iota((SUBS, LANES), 0)


def along_y(up, down, below, above):
    from_above = [
        jnp.where(subs() == SUBS - 1, above[f], pltpu.roll(up[f], SUBS - 1, 0)) for f in range(5)
    ]
    from_below = [jnp.where(subs() == 0, below[f], pltpu.roll(down[f], 1, 0)) for f in range(5)]
    return from_above, from_below


def along_z(up, down, below, above):
    from_above = [
        jnp.where(lanes() == LANES - 1, above[f], pltpu.roll(up[f], LANES - 1, 1)) for f in range(5)
    ]
    from_below = [jnp.where(lanes() == 0, below[f], pltpu.roll(down[f], 1, 1)) for f in range(5)]
    return from_above, from_below


HALO = 2
ABOVE = 3
FIRST_AT = 33
STRIP_AT = 70
MESSAGE_ROWS = 72


def row_of(u, g, xm, xp, f, row):
    own = g.shape[0] // SUBS
    place = row - HALO
    if place < 0:
        return xm[f * HALO + row]
    if place >= own:
        return xp[f * ABOVE + place - own]
    span = pl.ds(place * SUBS, SUBS)
    return u[f, span, :] if f < 5 else g[span, :]


def x_kernel(u, g, sp, x_low, x_high, kinds, semaphores):
    own = u.shape[1]
    moves = []
    for f in range(6):
        source = u.at[f] if f < 5 else g
        moves.append((source.at[pl.ds(0, ABOVE)], x_low.at[pl.ds(f * ABOVE, ABOVE)]))
        moves.append((source.at[pl.ds(own - HALO, HALO)], x_high.at[pl.ds(f * HALO, HALO)]))
    moves.append((sp.at[0], kinds))
    copies = [
        pltpu.make_async_copy(source, target, semaphores.at[k])
        for k, (source, target) in enumerate(moves)
    ]
    for copy in copies:
        copy.start()
    for copy in copies:
        copy.wait()
    x_low[6 * ABOVE] = kinds[...].astype(F32)


def strips(load, rows, parts):
    up, down, inner = parts
    for row in rows:
        value = load(row)
        here = lanes() // 2 == row
        up = jnp.where(here, pltpu.roll(value, 2 * row + 2, 1), up)
        down = jnp.where(here, pltpu.roll(value, 2 * row, 1) if row else value, down)
        inner = jnp.where(here, pltpu.roll(value, 2 * row + 1, 1), inner)
    return up, down, inner


def own_strips_kernel(u, g, *parts):
    own = g.shape[0] // SUBS
    for f in range(6):
        result = strips(
            lambda row: row_of(u, g, None, None, f, row),
            range(HALO, HALO + own),
            [jnp.ones((SUBS, LANES), F32)] * 3,
        )
        for part, value in zip(parts, result):
            part[f] = value


def all_strips_kernel(own, xm, xp, own_up, own_down, own_inner, *parts):
    for f in range(6):
        result = (own_up[f], own_down[f], own_inner[f])
        result = strips(lambda row: xm[f * HALO + row], range(HALO), result)
        result = strips(
            lambda row: xp[f * ABOVE + row - HALO - own],
            range(HALO + own, HALO + own + ABOVE),
            result,
        )
        for part, value in zip(parts, result):
            part[f] = value


def strips_of(zm, zp, f):
    odd = lanes() % 2 == 1
    first = jnp.where(odd, zm[f], zp[f])
    second = jnp.where(odd, pltpu.roll(zm[f], 1, 1), pltpu.roll(zp[f], LANES - 1, 1))
    return first, second


def y_kernel(u, g, xm, xp, zm, zp, partial, y_low, y_high, h):
    own = g.shape[0] // SUBS
    every = own + HALO + ABOVE
    odd = lanes() % 2 == 1
    ends = (lanes() == 0) | (lanes() == LANES - 1)
    first = [strips_of(zm, zp, f)[0] for f in range(6)]
    up, down = halves((2,), first)[0]
    for f in range(5):
        added = courant * jnp.where(odd, down[f], -up[f])
        for row in (0, every - 1):
            h[f, pl.ds(row * SUBS, SUBS), :] = jnp.ones((SUBS, LANES), F32)
        for row in range(1, every - 1):
            span = pl.ds(row * SUBS, SUBS)
            end = pltpu.roll(added, LANES - 1 - 2 * row, 1)
            h[f, span, :] = partial[f, span, :] + jnp.where(ends, end, 0.0)
    for f in range(6):
        for message, near in ((y_low, 0), (y_high, SUBS - 1)):
            for row in range(every):
                if HALO <= row < HALO + own:
                    continue
                line = row_of(u, g, xm, xp, f, row)[near : near + 1, :]
                message[f, pl.ds(FIRST_AT + row, 1), :] = line
            span = pl.ds(near, own, stride=SUBS)
            block = u[f, span, :] if f < 5 else g[span, :]
            message[f, pl.ds(FIRST_AT + HALO, own), :] = block
            if f < 5:
                message[f, pl.ds(0, own), :] = h[f, pl.ds(HALO * SUBS + near, own, stride=SUBS), :]
                last = (HALO + own) * SUBS + near
                message[f, pl.ds(own, 1), :] = h[f, pl.ds(last, 1), :]
            else:
                message[f, pl.ds(0, own + 1), :] = jnp.ones((own + 1, LANES), F32)
            strip = first[f][near : near + 1, :]
            message[f, pl.ds(STRIP_AT, 1), :] = strip
            message[f, pl.ds(STRIP_AT + 1, 1), :] = strip


def sweep(load, first, last, y_below, y_above, z_edge, finish):
    down = down_of(0, load(first - 1))
    pending = None
    for row in range(first, last + 1):
        cell = load(row)
        (x_up, x_down), (y_up, y_down), (z_up, z_down) = halves((0, 1, 2), cell)
        if pending is not None:
            finish(row - 1, [a + b for a, b in zip(pending, x_up)])
        if z_edge is None:
            edge = [0.0] * 5
        else:
            edge = [pltpu.roll(z_edge[f], LANES - 1 - 2 * row, 1) for f in range(5)]
        if y_below is None:
            below = above = [0.0] * 5
        else:
            below = [y_below[f, pl.ds(row, 1), :] for f in range(5)]
            above = [y_above[f, pl.ds(row, 1), :] for f in range(5)]
        core = total_change(
            cell,
            (along_y(y_up, y_down, below, above), along_z(z_up, z_down, edge, edge)),
        )
        pending = [a - b for a, b in zip(core, down)]
        down = x_down
    finish(last, [a + b for a, b in zip(pending, up_of(0, load(last + 1)))])


def lookup(density, species, tables):
    position = (density - density_low) * ((LUT - 1) / (density_high - density_low))
    knot = jnp.clip(jnp.floor(position), 0.0, LUT - 1.0)
    offset = position - knot
    lower_weight = jnp.maximum(0.0, 1.0 - jnp.abs(offset))
    upper_weight = jnp.maximum(0.0, 1.0 - jnp.abs(offset - 1.0))
    index = knot.astype(jnp.int32)
    lane_index = index % LANES
    bits = (index >= LANES, species % 2 == 1, species >= 2)

    def pick(table):
        values = [
            jnp.take_along_axis(table(k), lane_index, axis=1, mode="promise_in_bounds")
            for k in range(8)
        ]
        for bit in bits:
            values = [jnp.where(bit, values[k + 1], values[k]) for k in range(0, len(values), 2)]
        return values[0]

    def knots(channel):
        both = pick(lambda k: tables[channel, k])
        return (both & FIXED).astype(F32), lax.shift_right_logical(both, 16).astype(F32)

    result = []
    lower_scaled = lower_weight * (1.0 / FIXED)
    upper_scaled = upper_weight * (1.0 / FIXED)
    for channel in range(3):
        lower, upper = knots(channel)
        result.append(lower_scaled * lower + upper_scaled * upper)
    lower, upper = knots(3)
    scale = EXTINCTION_TOP / (FIXED * FIXED)
    result.append(
        (lower_weight * scale) * (lower * lower) + (upper_weight * scale) * (upper * upper)
    )
    return result


def classify(sp, xp, tables, properties, own):
    for place in range(own + 1):
        span = pl.ds(place * SUBS, SUBS)
        kind = sp[span, :] if place < own else xp[6 * ABOVE].astype(jnp.int32)
        found = lookup(properties[0, span, :], kind, tables)
        for channel in range(4):
            properties[channel, span, :] = found[channel]


def split_dot(value, weights):
    first = value.astype(jnp.bfloat16)
    rest = value - first.astype(F32)
    second = rest.astype(jnp.bfloat16)
    third = (rest - second.astype(F32)).astype(jnp.bfloat16)
    total = jnp.dot(first, weights, preferred_element_type=F32)
    total += jnp.dot(second, weights, preferred_element_type=F32)
    return total + jnp.dot(third, weights, preferred_element_type=F32)


def integrate(properties, grouped, rows, keep):
    extinction = properties[3]
    below = (iota((LANES, LANES), 0) < iota((LANES, LANES), 1)).astype(jnp.bfloat16)
    before = split_dot(extinction, below)
    factor = (1.0 - jnp.exp(-extinction)) * jnp.exp(-before)
    gathered = []
    for channel in range(4):
        if channel < 3:
            weighted = properties[channel] * factor
        else:
            weighted = extinction
        summed = jnp.sum(weighted, axis=1, keepdims=True)
        if channel == 3:
            summed = jnp.exp(-summed)
        plane = jnp.zeros((SUBS, LANES), F32)
        for row in range(rows):
            part = summed[row * SUBS : (row + 1) * SUBS]
            if row == rows - 1:
                part = part * keep + (1.0 - keep if channel == 3 else 0.0)
            plane = jnp.where(lanes() == row, part, plane)
        gathered.append(plane)
    following = [pltpu.roll(plane, LANES - 1, 1) for plane in gathered]
    block = jnp.concatenate(
        gathered + following + [jnp.zeros((LANES - 8 * SUBS, LANES), F32)], axis=0
    )
    grouped[...] = jnp.transpose(block)[: rows - 1]


def half_kernel(u, g, xm, xp, table_rows, h, tables):
    own = g.shape[0] // SUBS
    for k in range(32):
        tables[k // 8, k % 8] = jnp.broadcast_to(table_rows[pl.ds(k, 1), :], (SUBS, LANES))
    def at_first(row):
        return [row_of(u, g, xm, xp, f, row) for f in range(6)]

    def store_half(row, change):
        for f in range(5):
            h[f, pl.ds(row * SUBS, SUBS), :] = (
                row_of(u, g, xm, xp, f, row) - courant * change[f]
            )

    sweep(at_first, 1, HALO + own + 1, None, None, None, store_half)


def step_kernel(
    keep, u, g, sp, xm, xp, zm, zp, z_inner, y_low, y_high, ym, yp, partial, tables,
    grouped, h, y_below2, y_above2, z_edge2, y_below, y_above, properties
):
    own = g.shape[0] // SUBS
    odd = lanes() % 2 == 1

    for start in (1, 9, 17, 25, 28):
        span = pl.ds(FIRST_AT + start, SUBS)
        below = down_of(1, [ym[f, span, :] for f in range(6)])
        above = up_of(1, [yp[f, span, :] for f in range(6)])
        for f in range(5):
            y_below[f, pl.ds(start, SUBS), :] = courant * below[f]
            y_above[f, pl.ds(start, SUBS), :] = -courant * above[f]

    pairs = [strips_of(zm, zp, f) for f in range(6)]
    first = [pair[0] for pair in pairs]
    second = [pair[1] for pair in pairs]
    inner = [z_inner[f] for f in range(6)]
    corner = [
        jnp.where(
            subs() == 0,
            ym[f, pl.ds(STRIP_AT, 1), :],
            jnp.where(subs() == SUBS - 1, yp[f, pl.ds(STRIP_AT, 1), :], 1.0),
        )
        for f in range(6)
    ]
    corner_up, corner_down = halves((1,), corner)[0]
    (x_up, x_down), (y_up, y_down) = halves((0, 1), first)
    from_above = up_of(2, [jnp.where(odd, a, b) for a, b in zip(inner, second)])
    from_below = down_of(2, [jnp.where(odd, a, b) for a, b in zip(second, inner)])
    change = total_change(
        first,
        (
            (
                [pltpu.roll(q, LANES - 2, 1) for q in x_up],
                [pltpu.roll(q, 2, 1) for q in x_down],
            ),
            along_y(y_up, y_down, corner_down, corner_up),
            (from_above, from_below),
        ),
    )
    halfway = [first[f] - courant * change[f] for f in range(5)] + [first[5]]
    up, down = halves((2,), halfway)[0]
    for f in range(5):
        z_edge2[f] = jnp.where(odd, down[f], up[f])

    for start in (2, 10, 18, 26, 27):
        span = pl.ds(FIRST_AT + start, SUBS)
        before = pl.ds(start - HALO, SUBS)
        near = up_of(1, [y_low[f, span, :] for f in range(6)])
        halfway = [ym[f, before, :] - courant * near[f] for f in range(5)] + [ym[5, span, :]]
        part = down_of(1, halfway)
        near = down_of(1, [y_high[f, span, :] for f in range(6)])
        halfway = [yp[f, before, :] + courant * near[f] for f in range(5)] + [yp[5, span, :]]
        above = up_of(1, halfway)
        for f in range(5):
            y_below2[f, pl.ds(start, SUBS), :] = part[f]
            y_above2[f, pl.ds(start, SUBS), :] = above[f]

    for row in range(1, HALO + own + 2):
        span = pl.ds(row * SUBS, SUBS)
        for f in range(5):
            low = y_below[f, pl.ds(row, 1), :]
            high = y_above[f, pl.ds(row, 1), :]
            added = jnp.where(subs() == 0, low, jnp.where(subs() == SUBS - 1, high, 0.0))
            h[f, span, :] = partial[f, span, :] + added

    def finish(row, change):
        value = 0.5 * (
            row_of(u, g, xm, xp, 0, row) + h[0, pl.ds(row * SUBS, SUBS), :] - courant * change[0]
        )
        properties[0, pl.ds((row - HALO) * SUBS, SUBS), :] = value

    def at_half(row):
        return half_row(h, g, xm, xp, row)

    sweep(at_half, HALO, HALO + own, y_below2, y_above2, z_edge2, finish)
    classify(sp, xp, tables, properties, own)
    integrate(properties, grouped, own + 1, keep[0])


def half_row(h, g, xm, xp, row):
    return [h[f, pl.ds(row * SUBS, SUBS), :] for f in range(5)] + [
        row_of(None, g, xm, xp, 5, row)
    ]


def state_kernel(u, g, xm, xp, h, y_below2, y_above2, z_edge2, new):
    own = g.shape[0] // SUBS

    def finish(row, change):
        for f in range(5):
            before = row_of(u, g, xm, xp, f, row)
            new[f, pl.ds((row - HALO) * SUBS, SUBS), :] = 0.5 * (
                before + h[f, pl.ds(row * SUBS, SUBS), :] - courant * change[f]
            )

    def at_half(row):
        return half_row(h, g, xm, xp, row)

    sweep(at_half, HALO, HALO + own - 1, y_below2, y_above2, z_edge2, finish)


def image_kernel(across_y, across_z, parts, out):
    lane = iota((across_y, LANES), 1)
    channel = (lane // 8) % 4
    total = None
    for k in reversed(range(across_z)):
        part = parts[pl.ds(k, across_y, stride=across_z), :]
        through = part
        for c in range(3):
            moved = pltpu.roll(part, LANES - (24 - 8 * c), 1)
            through = jnp.where(channel == c, moved, through)
        if total is None:
            total = part
        else:
            total = jnp.where(channel == 3, 0.0, part) + through * total
    total = jnp.where(channel == 3, 1.0 - total, total)
    sub8 = iota((8, LANES), 0)
    lane8 = iota((8, LANES), 1)
    moved = jnp.zeros((8, LANES), F32)
    for k in range(across_y):
        wide = jnp.broadcast_to(total[k : k + 1, :], (8, LANES))
        shifted = wide
        for bit in range(3):
            amount = (LANES - (8 << bit)) % LANES
            shifted = jnp.where(
                (sub8 >> bit) & 1 == 1, pltpu.roll(shifted, amount, 1), shifted
            )
        if k:
            shifted = pltpu.roll(shifted, 8 * k, 1)
        moved = jnp.where(lane8 // 8 == k, shifted, moved)
    columns = 8 * across_y
    moved = jnp.where(lane8 < columns, moved, 0.0)
    screen = jnp.concatenate(
        [
            (1.0 - q / ZOOM) * moved[c : c + 1] + (q / ZOOM) * moved[4 + c : 5 + c]
            for c in range(4)
            for q in range(ZOOM)
        ],
        axis=0,
    )
    zoom = SW // columns
    for tile in range(SW // LANES):
        pixel = iota((8, LANES), 1) + tile * LANES
        whole = jnp.floor((pixel.astype(F32) + 0.5) * (1.0 / zoom))
        source = whole.astype(jnp.int32)
        offset = pixel.astype(F32) * (columns / SW) - whole
        lower = jnp.maximum(0.0, 1.0 - jnp.abs(offset))
        upper = jnp.maximum(0.0, 1.0 - jnp.abs(offset - 1.0))
        for half in range(2):
            block = screen[8 * half : 8 * half + 8]
            value = lower * jnp.take_along_axis(
                block, source, axis=1, mode="promise_in_bounds"
            ) + upper * jnp.take_along_axis(
                block, source + 1, axis=1, mode="promise_in_bounds"
            )
            for c in range(2):
                out[2 * half + c, :, pl.ds(tile * LANES, LANES)] = value[4 * c : 4 * c + 4]


def shifted(value, axis, steps):
    size = lax.axis_size(axis)
    return lax.ppermute(value, axis, [(i, (i + steps) % size) for i in range(size)])


def cost(size):
    return pl.CostEstimate(flops=size, bytes_accessed=size, transcendentals=0)


def struct(*shape):
    return jax.ShapeDtypeStruct(shape, F32)


def local(conserved, gamma_field, species, lut_color, lut_extinction):
    rows = conserved.shape[1]
    cells = rows * SUBS
    params = pltpu.CompilerParams(vmem_limit_bytes=VMEM_LIMIT)
    across_y = lax.axis_size("gy")
    across_z = lax.axis_size("gz")

    roots = jnp.sqrt(jnp.clip(lut_extinction, 0.0, EXTINCTION_TOP) * (1.0 / EXTINCTION_TOP))
    values = jnp.concatenate([jnp.clip(lut_color, 0.0, 1.0), roots[:, None, :]], axis=1)
    fixed = jnp.round(values * FIXED).astype(jnp.int32)
    following = jnp.pad(fixed[:, :, 1:], ((0, 0), (0, 0), (0, 1)))
    table_rows = (fixed + lax.shift_left(following, 16)).transpose(1, 0, 2).reshape(32, LANES)

    in_hbm = pl.BlockSpec(memory_space=pltpu.HBM)
    x_low, x_high = pl.pallas_call(
        x_kernel,
        out_shape=(struct(6 * ABOVE + 1, SUBS, LANES), struct(6 * HALO, SUBS, LANES)),
        in_specs=[in_hbm, in_hbm, in_hbm],
        scratch_shapes=[pltpu.VMEM((SUBS, LANES), jnp.int32), pltpu.SemaphoreType.DMA((13,))],
        compiler_params=pltpu.CompilerParams(vmem_limit_bytes=VMEM_LIMIT),
        name="x_layers",
    )(*[pltpu.with_memory_space_constraint(q, pltpu.HBM) for q in (conserved, gamma_field, species)])
    x_low, x_high, conserved, gamma_field = lax.optimization_barrier(
        (x_low, x_high, conserved, gamma_field)
    )
    xm = shifted(x_high, "gx", 1)
    xp = shifted(x_low, "gx", -1)
    brick = (
        conserved.reshape(5, cells, LANES),
        gamma_field.reshape(cells, LANES),
    )
    strip = struct(6, SUBS, LANES)
    own_parts = pl.pallas_call(
        own_strips_kernel,
        out_shape=(strip, strip, strip),
        compiler_params=params,
        cost_estimate=cost(2_000_000),
        name="own_strips",
    )(*brick)
    z_up, z_down, z_inner = pl.pallas_call(
        functools.partial(all_strips_kernel, rows),
        out_shape=(strip, strip, strip),
        compiler_params=params,
        name="strips",
    )(xm, xp, *own_parts)
    zm = shifted(z_up, "gz", 1)
    zp = shifted(z_down, "gz", -1)
    every = cells + (HALO + ABOVE) * SUBS
    partial, tables = pl.pallas_call(
        half_kernel,
        out_shape=(
            struct(5, every, LANES),
            jax.ShapeDtypeStruct((4, 8, SUBS, LANES), jnp.int32),
        ),
        compiler_params=params,
        cost_estimate=cost(4_000_000),
        name="half",
    )(*brick, xm, xp, table_rows)
    message = struct(6, MESSAGE_ROWS, LANES)
    y_low, y_high, partial = pl.pallas_call(
        y_kernel,
        out_shape=(message, message, struct(5, every, LANES)),
        compiler_params=params,
        name="layers",
    )(*brick, xm, xp, zm, zp, partial)
    ym = shifted(y_high, "gy", 1)
    yp = shifted(y_low, "gy", -1)
    layer = pltpu.VMEM((5, 40, LANES), F32)
    place = lax.axis_index("gx")
    keep = jnp.where(place == lax.axis_size("gx") - 1, 0.0, 1.0).reshape(1)
    vmem = pl.BlockSpec(memory_space=pltpu.VMEM)
    grouped, *halves_found = pl.pallas_call(
        step_kernel,
        in_specs=[pl.BlockSpec(memory_space=pltpu.SMEM)] + [vmem] * 14,
        out_shape=(
            struct(rows, LANES),
            struct(5, every, LANES),
            struct(5, 40, LANES),
            struct(5, 40, LANES),
            struct(5, SUBS, LANES),
        ),
        scratch_shapes=[
            layer,
            layer,
            pltpu.VMEM((4, cells + SUBS, LANES), F32),
        ],
        compiler_params=params,
        name="density",
    )(
        keep,
        *brick,
        species.reshape(cells, LANES),
        xm,
        xp,
        zm,
        zp,
        z_inner,
        y_low,
        y_high,
        ym,
        yp,
        partial,
        tables,
    )
    new_state = pl.pallas_call(
        state_kernel,
        out_shape=struct(5, cells, LANES),
        compiler_params=params,
        cost_estimate=cost(6_000_000),
        name="state",
    )(*brick, xm, xp, *halves_found)
    merged = lax.all_to_all(
        grouped.reshape(across_y * across_z, 1, LANES), ("gy", "gz"), 0, 0, tiled=True
    ).reshape(across_y * across_z, LANES)
    image = pl.pallas_call(
        functools.partial(image_kernel, across_y, across_z),
        out_shape=struct(4, ZOOM, SW),
        compiler_params=params,
        name="image",
    )(merged)
    return new_state.reshape(conserved.shape), image


def solution(mesh):
    return jax.shard_map(
        local,
        mesh=mesh,
        in_specs=(P(None, "gx", "gy", "gz"), P("gx", "gy", "gz"), P("gx", "gy", "gz"), P(), P()),
        out_specs=(P(None, "gx", "gy", "gz"), P(None, ("gx", "gy", "gz"), None)),
        check_vma=False,
    )
```

```python
import functools

import jax
import jax.numpy as jnp
from jax import lax
from jax.experimental import pallas as pl
from jax.experimental.pallas import tpu as pltpu
from jax.sharding import PartitionSpec as P

SW = 1920
ZOOM = 4
CLASSES = 4
LUT = 256
FIXED = 65535
EXTINCTION_TOP = 0.01

dissipation = 3.0
courant = 0.11
density_low = 0.6
density_high = 1.6

F32 = jnp.float32
LANES = 128
SUBS = 8
VMEM_LIMIT = 51 * 1024 * 1024


def iota(shape, dim):
    return lax.broadcasted_iota(jnp.int32, shape, dim)


def halves(direction, cell):
    density, m1, m2, m3, energy, gamma = cell
    momenta = (m1, m2, m3)
    inverse = 1.0 / density
    kinetic = 0.5 * (m1 * m1 + m2 * m2 + m3 * m3) * inverse
    pressure = (gamma - 1.0) * (energy - kinetic)
    half_p = 0.5 * pressure
    scaled = [(0.5 * dissipation) * q for q in (density, m1, m2, m3, energy)]
    result = []
    for d in direction:
        half_v = 0.5 * momenta[d] * inverse
        flux = [0.5 * momenta[d]]
        for member in range(3):
            component = momenta[member] * half_v
            flux.append(component + half_p if member == d else component)
        flux.append((energy + pressure) * half_v)
        result.append(
            ([a - b for a, b in zip(flux, scaled)], [a + b for a, b in zip(flux, scaled)])
        )
    return result


def up_of(direction, cell):
    return halves((direction,), cell)[0][0]


def down_of(direction, cell):
    return halves((direction,), cell)[0][1]


def total_change(cell, pairs):
    result = []
    for f in range(5):
        total = (6.0 * 0.5 * dissipation) * cell[f]
        for above, below in pairs:
            total = total + (above[f] - below[f])
        result.append(total)
    return result


def lanes():
    return iota((SUBS, LANES), 1)


def subs():
    return iota((SUBS, LANES), 0)


def along_y(up, down, below, above):
    from_above = [
        jnp.where(subs() == SUBS - 1, above[f], pltpu.roll(up[f], SUBS - 1, 0)) for f in range(5)
    ]
    from_below = [jnp.where(subs() == 0, below[f], pltpu.roll(down[f], 1, 0)) for f in range(5)]
    return from_above, from_below


def along_z(up, down, below, above):
    from_above = [
        jnp.where(lanes() == LANES - 1, above[f], pltpu.roll(up[f], LANES - 1, 1)) for f in range(5)
    ]
    from_below = [jnp.where(lanes() == 0, below[f], pltpu.roll(down[f], 1, 1)) for f in range(5)]
    return from_above, from_below


HALO = 2
ABOVE = 3
FIRST_AT = 33
STRIP_AT = 70
MESSAGE_ROWS = 72


def row_of(u, g, xm, xp, f, row):
    own = g.shape[0] // SUBS
    place = row - HALO
    if place < 0:
        return xm[f * HALO + row]
    if place >= own:
        return xp[f * ABOVE + place - own]
    span = pl.ds(place * SUBS, SUBS)
    return u[f, span, :] if f < 5 else g[span, :]


def x_kernel(u, g, sp, x_low, x_high, kinds, semaphores):
    own = u.shape[1]
    moves = []
    for f in range(6):
        source = u.at[f] if f < 5 else g
        moves.append((source.at[pl.ds(0, ABOVE)], x_low.at[pl.ds(f * ABOVE, ABOVE)]))
        moves.append((source.at[pl.ds(own - HALO, HALO)], x_high.at[pl.ds(f * HALO, HALO)]))
    moves.append((sp.at[0], kinds))
    copies = [
        pltpu.make_async_copy(source, target, semaphores.at[k])
        for k, (source, target) in enumerate(moves)
    ]
    for copy in copies:
        copy.start()
    for copy in copies:
        copy.wait()
    x_low[6 * ABOVE] = kinds[...].astype(F32)


def strips(load, rows, parts):
    up, down, inner = parts
    for row in rows:
        value = load(row)
        here = lanes() // 2 == row
        up = jnp.where(here, pltpu.roll(value, 2 * row + 2, 1), up)
        down = jnp.where(here, pltpu.roll(value, 2 * row, 1) if row else value, down)
        inner = jnp.where(here, pltpu.roll(value, 2 * row + 1, 1), inner)
    return up, down, inner


def own_strips_kernel(u, g, *parts):
    own = g.shape[0] // SUBS
    for f in range(6):
        result = strips(
            lambda row: row_of(u, g, None, None, f, row),
            range(HALO, HALO + own),
            [jnp.ones((SUBS, LANES), F32)] * 3,
        )
        for part, value in zip(parts, result):
            part[f] = value


def all_strips_kernel(own, xm, xp, own_up, own_down, own_inner, *parts):
    for f in range(6):
        result = (own_up[f], own_down[f], own_inner[f])
        result = strips(lambda row: xm[f * HALO + row], range(HALO), result)
        result = strips(
            lambda row: xp[f * ABOVE + row - HALO - own],
            range(HALO + own, HALO + own + ABOVE),
            result,
        )
        for part, value in zip(parts, result):
            part[f] = value


def strips_of(zm, zp, f):
    odd = lanes() % 2 == 1
    first = jnp.where(odd, zm[f], zp[f])
    second = jnp.where(odd, pltpu.roll(zm[f], 1, 1), pltpu.roll(zp[f], LANES - 1, 1))
    return first, second


def y_kernel(u, g, xm, xp, zm, zp, partial, y_low, y_high, h, strip_pairs):
    own = g.shape[0] // SUBS
    every = own + HALO + ABOVE
    odd = lanes() % 2 == 1
    ends = (lanes() == 0) | (lanes() == LANES - 1)
    first = []
    for f in range(6):
        near, far = strips_of(zm, zp, f)
        first.append(near)
        strip_pairs[f] = near
        strip_pairs[6 + f] = far
    up, down = halves((2,), first)[0]
    for f in range(5):
        added = courant * jnp.where(odd, down[f], -up[f])
        for row in (0, every - 1):
            h[f, pl.ds(row * SUBS, SUBS), :] = jnp.ones((SUBS, LANES), F32)
        for row in range(1, every - 1):
            span = pl.ds(row * SUBS, SUBS)
            end = pltpu.roll(added, LANES - 1 - 2 * row, 1)
            h[f, span, :] = partial[f, span, :] + jnp.where(ends, end, 0.0)
    for f in range(6):
        for message, near in ((y_low, 0), (y_high, SUBS - 1)):
            for row in range(every):
                if HALO <= row < HALO + own:
                    continue
                line = row_of(u, g, xm, xp, f, row)[near : near + 1, :]
                message[f, pl.ds(FIRST_AT + row, 1), :] = line
            span = pl.ds(near, own, stride=SUBS)
            block = u[f, span, :] if f < 5 else g[span, :]
            message[f, pl.ds(FIRST_AT + HALO, own), :] = block
            if f < 5:
                message[f, pl.ds(0, own), :] = h[f, pl.ds(HALO * SUBS + near, own, stride=SUBS), :]
                last = (HALO + own) * SUBS + near
                message[f, pl.ds(own, 1), :] = h[f, pl.ds(last, 1), :]
            else:
                message[f, pl.ds(0, own + 1), :] = jnp.ones((own + 1, LANES), F32)
            strip = first[f][near : near + 1, :]
            message[f, pl.ds(STRIP_AT, 1), :] = strip
            message[f, pl.ds(STRIP_AT + 1, 1), :] = strip


def sweep(load, first, last, y_below, y_above, z_edge, finish):
    down = down_of(0, load(first - 1))
    pending = None
    for row in range(first, last + 1):
        cell = load(row)
        (x_up, x_down), (y_up, y_down), (z_up, z_down) = halves((0, 1, 2), cell)
        if pending is not None:
            finish(row - 1, [a + b for a, b in zip(pending, x_up)])
        if z_edge is None:
            edge = [0.0] * 5
        else:
            edge = [pltpu.roll(z_edge[f], LANES - 1 - 2 * row, 1) for f in range(5)]
        if y_below is None:
            below = above = [0.0] * 5
        else:
            below = [y_below[f, pl.ds(row, 1), :] for f in range(5)]
            above = [y_above[f, pl.ds(row, 1), :] for f in range(5)]
        core = total_change(
            cell,
            (along_y(y_up, y_down, below, above), along_z(z_up, z_down, edge, edge)),
        )
        pending = [a - b for a, b in zip(core, down)]
        down = x_down
    finish(last, [a + b for a, b in zip(pending, up_of(0, load(last + 1)))])


def lookup(density, species, tables):
    position = (density - density_low) * ((LUT - 1) / (density_high - density_low))
    knot = jnp.clip(jnp.floor(position), 0.0, LUT - 1.0)
    offset = position - knot
    lower_weight = jnp.maximum(0.0, 1.0 - jnp.abs(offset))
    upper_weight = jnp.maximum(0.0, 1.0 - jnp.abs(offset - 1.0))
    index = knot.astype(jnp.int32)
    lane_index = index % LANES
    bits = (index >= LANES, species % 2 == 1, species >= 2)

    def pick(table):
        values = [
            jnp.take_along_axis(table(k), lane_index, axis=1, mode="promise_in_bounds")
            for k in range(8)
        ]
        for bit in bits:
            values = [jnp.where(bit, values[k + 1], values[k]) for k in range(0, len(values), 2)]
        return values[0]

    def knots(channel):
        both = pick(lambda k: tables[channel, k])
        return (both & FIXED).astype(F32), lax.shift_right_logical(both, 16).astype(F32)

    result = []
    lower_scaled = lower_weight * (1.0 / FIXED)
    upper_scaled = upper_weight * (1.0 / FIXED)
    for channel in range(3):
        lower, upper = knots(channel)
        result.append(lower_scaled * lower + upper_scaled * upper)
    lower, upper = knots(3)
    scale = EXTINCTION_TOP / (FIXED * FIXED)
    result.append(
        (lower_weight * scale) * (lower * lower) + (upper_weight * scale) * (upper * upper)
    )
    return result


def classify(sp, xp, tables, properties, own):
    for place in range(own + 1):
        span = pl.ds(place * SUBS, SUBS)
        kind = sp[span, :] if place < own else xp[6 * ABOVE].astype(jnp.int32)
        found = lookup(properties[0, span, :], kind, tables)
        for channel in range(4):
            properties[channel, span, :] = found[channel]


def split_dot(value, weights):
    first = value.astype(jnp.bfloat16)
    rest = value - first.astype(F32)
    second = rest.astype(jnp.bfloat16)
    third = (rest - second.astype(F32)).astype(jnp.bfloat16)
    total = jnp.dot(first, weights, preferred_element_type=F32)
    total += jnp.dot(second, weights, preferred_element_type=F32)
    return total + jnp.dot(third, weights, preferred_element_type=F32)


def integrate(properties, grouped, rows, keep):
    extinction = properties[3]
    below = (iota((LANES, LANES), 0) < iota((LANES, LANES), 1)).astype(jnp.bfloat16)
    before = split_dot(extinction, below)
    factor = (1.0 - jnp.exp(-extinction)) * jnp.exp(-before)
    gathered = []
    for channel in range(4):
        if channel < 3:
            weighted = properties[channel] * factor
        else:
            weighted = extinction
        summed = jnp.sum(weighted, axis=1, keepdims=True)
        if channel == 3:
            summed = jnp.exp(-summed)
        plane = jnp.zeros((SUBS, LANES), F32)
        for row in range(rows):
            part = summed[row * SUBS : (row + 1) * SUBS]
            if row == rows - 1:
                part = part * keep + (1.0 - keep if channel == 3 else 0.0)
            plane = jnp.where(lanes() == row, part, plane)
        gathered.append(plane)
    following = [pltpu.roll(plane, LANES - 1, 1) for plane in gathered]
    block = jnp.concatenate(
        gathered + following + [jnp.zeros((LANES - 8 * SUBS, LANES), F32)], axis=0
    )
    grouped[...] = jnp.transpose(block)[: rows - 1]


def half_kernel(u, g, xm, xp, table_rows, h, tables):
    own = g.shape[0] // SUBS
    for k in range(32):
        tables[k // 8, k % 8] = jnp.broadcast_to(table_rows[pl.ds(k, 1), :], (SUBS, LANES))
    def at_first(row):
        return [row_of(u, g, xm, xp, f, row) for f in range(6)]

    def store_half(row, change):
        for f in range(5):
            h[f, pl.ds(row * SUBS, SUBS), :] = (
                row_of(u, g, xm, xp, f, row) - courant * change[f]
            )

    sweep(at_first, 1, HALO + own + 1, None, None, None, store_half)


def step_kernel(
    keep, u, g, sp, xm, xp, strip_pairs, z_inner, y_low, y_high, ym, yp, partial, tables,
    grouped, h, y_below2, y_above2, z_edge2, y_below, y_above, properties
):
    own = g.shape[0] // SUBS
    odd = lanes() % 2 == 1

    for start in (1, 9, 17, 25, 28):
        span = pl.ds(FIRST_AT + start, SUBS)
        below = down_of(1, [ym[f, span, :] for f in range(6)])
        above = up_of(1, [yp[f, span, :] for f in range(6)])
        for f in range(5):
            y_below[f, pl.ds(start, SUBS), :] = courant * below[f]
            y_above[f, pl.ds(start, SUBS), :] = -courant * above[f]

    first = [strip_pairs[f] for f in range(6)]
    second = [strip_pairs[6 + f] for f in range(6)]
    inner = [z_inner[f] for f in range(6)]
    corner = [
        jnp.where(
            subs() == 0,
            ym[f, pl.ds(STRIP_AT, 1), :],
            jnp.where(subs() == SUBS - 1, yp[f, pl.ds(STRIP_AT, 1), :], 1.0),
        )
        for f in range(6)
    ]
    corner_up, corner_down = halves((1,), corner)[0]
    (x_up, x_down), (y_up, y_down) = halves((0, 1), first)
    from_above = up_of(2, [jnp.where(odd, a, b) for a, b in zip(inner, second)])
    from_below = down_of(2, [jnp.where(odd, a, b) for a, b in zip(second, inner)])
    change = total_change(
        first,
        (
            (
                [pltpu.roll(q, LANES - 2, 1) for q in x_up],
                [pltpu.roll(q, 2, 1) for q in x_down],
            ),
            along_y(y_up, y_down, corner_down, corner_up),
            (from_above, from_below),
        ),
    )
    halfway = [first[f] - courant * change[f] for f in range(5)] + [first[5]]
    up, down = halves((2,), halfway)[0]
    for f in range(5):
        z_edge2[f] = jnp.where(odd, down[f], up[f])

    for start in (2, 10, 18, 26, 27):
        span = pl.ds(FIRST_AT + start, SUBS)
        before = pl.ds(start - HALO, SUBS)
        near = up_of(1, [y_low[f, span, :] for f in range(6)])
        halfway = [ym[f, before, :] - courant * near[f] for f in range(5)] + [ym[5, span, :]]
        part = down_of(1, halfway)
        near = down_of(1, [y_high[f, span, :] for f in range(6)])
        halfway = [yp[f, before, :] + courant * near[f] for f in range(5)] + [yp[5, span, :]]
        above = up_of(1, halfway)
        for f in range(5):
            y_below2[f, pl.ds(start, SUBS), :] = part[f]
            y_above2[f, pl.ds(start, SUBS), :] = above[f]

    for row in range(1, HALO + own + 2):
        span = pl.ds(row * SUBS, SUBS)
        for f in range(5):
            low = y_below[f, pl.ds(row, 1), :]
            high = y_above[f, pl.ds(row, 1), :]
            added = jnp.where(subs() == 0, low, jnp.where(subs() == SUBS - 1, high, 0.0))
            h[f, span, :] = partial[f, span, :] + added

    def finish(row, change):
        value = 0.5 * (
            row_of(u, g, xm, xp, 0, row) + h[0, pl.ds(row * SUBS, SUBS), :] - courant * change[0]
        )
        properties[0, pl.ds((row - HALO) * SUBS, SUBS), :] = value

    def at_half(row):
        return half_row(h, g, xm, xp, row)

    sweep(at_half, HALO, HALO + own, y_below2, y_above2, z_edge2, finish)
    classify(sp, xp, tables, properties, own)
    integrate(properties, grouped, own + 1, keep[0])


def half_row(h, g, xm, xp, row):
    return [h[f, pl.ds(row * SUBS, SUBS), :] for f in range(5)] + [
        row_of(None, g, xm, xp, 5, row)
    ]


def state_kernel(u, g, xm, xp, h, y_below2, y_above2, z_edge2, new):
    own = g.shape[0] // SUBS

    def finish(row, change):
        for f in range(5):
            before = row_of(u, g, xm, xp, f, row)
            new[f, pl.ds((row - HALO) * SUBS, SUBS), :] = 0.5 * (
                before + h[f, pl.ds(row * SUBS, SUBS), :] - courant * change[f]
            )

    def at_half(row):
        return half_row(h, g, xm, xp, row)

    sweep(at_half, HALO, HALO + own - 1, y_below2, y_above2, z_edge2, finish)


def image_kernel(across_y, across_z, parts, out):
    lane = iota((across_y, LANES), 1)
    channel = (lane // 8) % 4
    total = None
    for k in reversed(range(across_z)):
        part = parts[pl.ds(k, across_y, stride=across_z), :]
        through = part
        for c in range(3):
            moved = pltpu.roll(part, LANES - (24 - 8 * c), 1)
            through = jnp.where(channel == c, moved, through)
        if total is None:
            total = part
        else:
            total = jnp.where(channel == 3, 0.0, part) + through * total
    total = jnp.where(channel == 3, 1.0 - total, total)
    sub8 = iota((8, LANES), 0)
    lane8 = iota((8, LANES), 1)
    moved = jnp.zeros((8, LANES), F32)
    for k in range(across_y):
        wide = jnp.broadcast_to(total[k : k + 1, :], (8, LANES))
        shifted = wide
        for bit in range(3):
            amount = (LANES - (8 << bit)) % LANES
            shifted = jnp.where(
                (sub8 >> bit) & 1 == 1, pltpu.roll(shifted, amount, 1), shifted
            )
        if k:
            shifted = pltpu.roll(shifted, 8 * k, 1)
        moved = jnp.where(lane8 // 8 == k, shifted, moved)
    columns = 8 * across_y
    moved = jnp.where(lane8 < columns, moved, 0.0)
    screen = jnp.concatenate(
        [
            (1.0 - q / ZOOM) * moved[c : c + 1] + (q / ZOOM) * moved[4 + c : 5 + c]
            for c in range(4)
            for q in range(ZOOM)
        ],
        axis=0,
    )
    zoom = SW // columns
    for tile in range(SW // LANES):
        pixel = iota((8, LANES), 1) + tile * LANES
        whole = jnp.floor((pixel.astype(F32) + 0.5) * (1.0 / zoom))
        source = whole.astype(jnp.int32)
        offset = pixel.astype(F32) * (columns / SW) - whole
        lower = jnp.maximum(0.0, 1.0 - jnp.abs(offset))
        upper = jnp.maximum(0.0, 1.0 - jnp.abs(offset - 1.0))
        for half in range(2):
            block = screen[8 * half : 8 * half + 8]
            value = lower * jnp.take_along_axis(
                block, source, axis=1, mode="promise_in_bounds"
            ) + upper * jnp.take_along_axis(
                block, source + 1, axis=1, mode="promise_in_bounds"
            )
            for c in range(2):
                out[2 * half + c, :, pl.ds(tile * LANES, LANES)] = value[4 * c : 4 * c + 4]


def shifted(value, axis, steps):
    size = lax.axis_size(axis)
    return lax.ppermute(value, axis, [(i, (i + steps) % size) for i in range(size)])


def cost(size):
    return pl.CostEstimate(flops=size, bytes_accessed=size, transcendentals=0)


def struct(*shape):
    return jax.ShapeDtypeStruct(shape, F32)


def kept(*shape):
    return pltpu.VMEM(shape, F32)


def local(conserved, gamma_field, species, lut_color, lut_extinction):
    rows = conserved.shape[1]
    cells = rows * SUBS
    params = pltpu.CompilerParams(vmem_limit_bytes=VMEM_LIMIT)
    across_y = lax.axis_size("gy")
    across_z = lax.axis_size("gz")

    roots = jnp.sqrt(jnp.clip(lut_extinction, 0.0, EXTINCTION_TOP) * (1.0 / EXTINCTION_TOP))
    values = jnp.concatenate([jnp.clip(lut_color, 0.0, 1.0), roots[:, None, :]], axis=1)
    fixed = jnp.round(values * FIXED).astype(jnp.int32)
    following = jnp.pad(fixed[:, :, 1:], ((0, 0), (0, 0), (0, 1)))
    table_rows = (fixed + lax.shift_left(following, 16)).transpose(1, 0, 2).reshape(32, LANES)

    in_hbm = pl.BlockSpec(memory_space=pltpu.HBM)
    x_low, x_high = pl.pallas_call(
        x_kernel,
        out_shape=(struct(6 * ABOVE + 1, SUBS, LANES), struct(6 * HALO, SUBS, LANES)),
        in_specs=[in_hbm, in_hbm, in_hbm],
        scratch_shapes=[pltpu.VMEM((SUBS, LANES), jnp.int32), pltpu.SemaphoreType.DMA((13,))],
        compiler_params=pltpu.CompilerParams(vmem_limit_bytes=VMEM_LIMIT),
        name="x_layers",
    )(*[pltpu.with_memory_space_constraint(q, pltpu.HBM) for q in (conserved, gamma_field, species)])
    x_low, x_high, conserved, gamma_field = lax.optimization_barrier(
        (x_low, x_high, conserved, gamma_field)
    )
    xm = shifted(x_high, "gx", 1)
    xp = shifted(x_low, "gx", -1)
    brick = (
        conserved.reshape(5, cells, LANES),
        gamma_field.reshape(cells, LANES),
    )
    strip = struct(6, SUBS, LANES)
    own_parts = pl.pallas_call(
        own_strips_kernel,
        out_shape=(strip, strip, strip),
        compiler_params=params,
        cost_estimate=cost(2_000_000),
        name="own_strips",
    )(*brick)
    z_up, z_down, z_inner = pl.pallas_call(
        functools.partial(all_strips_kernel, rows),
        out_shape=(strip, strip, kept(6, SUBS, LANES)),
        compiler_params=params,
        name="strips",
    )(xm, xp, *own_parts)
    zm = shifted(z_up, "gz", 1)
    zp = shifted(z_down, "gz", -1)
    every = cells + (HALO + ABOVE) * SUBS
    partial, tables = pl.pallas_call(
        half_kernel,
        out_shape=(
            kept(5, every, LANES),
            pltpu.VMEM((4, 8, SUBS, LANES), jnp.int32),
        ),
        compiler_params=params,
        cost_estimate=cost(4_000_000),
        name="half",
    )(*brick, xm, xp, table_rows)
    message = struct(6, MESSAGE_ROWS, LANES)
    y_low, y_high, partial, strip_pairs = pl.pallas_call(
        y_kernel,
        out_shape=(message, message, kept(5, every, LANES), kept(12, SUBS, LANES)),
        compiler_params=params,
        name="layers",
    )(*brick, xm, xp, zm, zp, partial)
    ym = shifted(y_high, "gy", 1)
    yp = shifted(y_low, "gy", -1)
    layer = pltpu.VMEM((5, 40, LANES), F32)
    place = lax.axis_index("gx")
    keep = jnp.where(place == lax.axis_size("gx") - 1, 0.0, 1.0).reshape(1)
    vmem = pl.BlockSpec(memory_space=pltpu.VMEM)
    grouped, *halves_found = pl.pallas_call(
        step_kernel,
        in_specs=[pl.BlockSpec(memory_space=pltpu.SMEM)] + [vmem] * 13,
        out_shape=(
            kept(rows, LANES),
            kept(5, every, LANES),
            kept(5, 40, LANES),
            kept(5, 40, LANES),
            kept(5, SUBS, LANES),
        ),
        scratch_shapes=[
            layer,
            layer,
            pltpu.VMEM((4, cells + SUBS, LANES), F32),
        ],
        compiler_params=params,
        name="density",
    )(
        keep,
        *brick,
        species.reshape(cells, LANES),
        xm,
        xp,
        strip_pairs,
        z_inner,
        y_low,
        y_high,
        ym,
        yp,
        partial,
        tables,
    )
    new_state = pl.pallas_call(
        state_kernel,
        out_shape=struct(5, cells, LANES),
        compiler_params=params,
        cost_estimate=cost(6_000_000),
        name="state",
    )(*brick, xm, xp, *halves_found)
    merged = lax.all_to_all(
        grouped.reshape(across_y * across_z, 1, LANES), ("gy", "gz"), 0, 0, tiled=True
    ).reshape(across_y * across_z, LANES)
    image = pl.pallas_call(
        functools.partial(image_kernel, across_y, across_z),
        out_shape=struct(4, ZOOM, SW),
        compiler_params=params,
        name="image",
    )(merged)
    return new_state.reshape(conserved.shape), image


def solution(mesh):
    return jax.shard_map(
        local,
        mesh=mesh,
        in_specs=(P(None, "gx", "gy", "gz"), P("gx", "gy", "gz"), P("gx", "gy", "gz"), P(), P()),
        out_specs=(P(None, "gx", "gy", "gz"), P(None, ("gx", "gy", "gz"), None)),
        check_vma=False,
    )
```
